32 devices in a mesh: rep: 2 (over y), cell: 4 (over x, core), gene: 4 (over z).
Axes of the slice: x: 2, y: 2, z: 4, core: 2. Of those that a mesh axis runs over, the one named last changes fastest.
Arguments:
- counts: int32 [4096, 5120], P('cell', 'gene'), may hold values from 0 to 63
- usage_init: float32 [8192, 200], P(('rep', 'cell')), parts along dimension 0, may hold values from 0.05 to 1
- program_init: float32 [400, 5120], P('rep', 'gene'), parts along dimension 0, may hold values from 0.05 to 1
Outputs:
- usage: float32 [8192, 200], P(('rep', 'cell')), parts along dimension 0
- program: float32 [400, 5120], P('rep', 'gene'), parts along dimension 0
The draws below stay inside these ranges and needn't reach their ends.
There are 2 independent parts, one for each index of `rep`. The reference program is written for one: setup_inputs(seed, part) draws one part's arguments, and reference() takes and returns one part's arrays. A program takes and returns all parts, laid end to end along the dimension named above; an argument that names none is the same for every part. Nothing has to cross between parts.
All inputs are finite; a program needn't handle non-finite values.
Results may differ from the reference program's by a relative error of at most 0.0001.
Values sent between devices are 32-bit elements; how exact they have to be, the bound alone decides.
No kernel may reach another device: no remote copies, remote signals or barrier semaphores. Data moves between devices by JAX's collectives and lax.ppermute only.
A program may use at most 64 MiB of HBM per device.

```python
import math
import jax
import jax.numpy as jnp
import numpy as np
from jax import lax

GENES = 5120
K = 200
ITERS = 2
CELLS = 4096


def set_ends(entries, stream_key, low, high):
    shape = entries.shape
    index_at = [jax.random.randint(jax.random.fold_in(stream_key, axis), (), 0, shape[axis]) for axis in range(len(shape))]
    entries = entries.at[tuple(index_at)].set(low)
    longest = shape.index(max(shape))
    index_at[longest] = (index_at[longest] + 1) % shape[longest]
    return entries.at[tuple(index_at)].set(high)


def level_of(key, dims, pieces, least, high):
    factor_of, own = 1.0, jax.random.fold_in(key, 6)
    for axis_at, parts in pieces:
        draws = jnp.exp(jax.random.uniform(jax.random.fold_in(own, axis_at), (parts,), jnp.float32, least / len(pieces), high / len(pieces)))
        factor_of = factor_of * jnp.repeat(draws, dims[axis_at] // parts).reshape([-1 if axis == axis_at else 1 for axis in range(len(dims))])
    return factor_of


def rank_bounds(number_of, lean):
    portions = [(1 << 20) // math.isqrt(grade ** lean) + 1 for grade in range(1, number_of + 1)]
    scale = 1 + sum(portions) // (1 << 30)
    return np.cumsum(np.array([max(1, weight // scale) for weight in portions]))


def skewed_ids(rng, dims, number_of, skew):
    grid = rank_bounds(number_of, skew)
    pick = jax.random.randint(jax.random.fold_in(rng, 1), dims, 0, int(grid[number_of - 1]))
    standing = jnp.searchsorted(jnp.asarray(grid, jnp.int32), pick, side="right")
    return jax.random.permutation(jax.random.fold_in(rng, 2), number_of)[standing].astype(jnp.int32)


def setup_inputs(seed: int = 0, part: int = 0) -> dict:
    keys = jax.random.split(jax.random.key(seed), 4)
    part_splits = jax.random.split(jax.random.fold_in(keys[3], part), 4)
    counts = set_ends(skewed_ids(keys[0], (CELLS, GENES), 64, 2), jax.random.fold_in(keys[0], 3), 0, 63).astype(jnp.int32)
    usage_init = jnp.clip(jnp.exp(math.log(1.0) - 2.9957323 * jax.random.uniform(part_splits[1], (CELLS, K), jnp.float32) ** level_of(part_splits[1], (CELLS, K), ((0, 4),), -0.2, 0.2)), 0.05, 1.0)
    program_init = jnp.clip(jnp.exp(math.log(1.0) - 2.9957323 * jax.random.uniform(part_splits[2], (K, GENES), jnp.float32) ** level_of(part_splits[2], (K, GENES), ((1, 4),), -0.2, 0.2)), 0.05, 1.0)
    return dict(counts=counts, usage_init=usage_init, program_init=program_init)


def reference(counts, usage_init, program_init):
    highest = lax.Precision.HIGHEST
    expression = counts.astype(jnp.float32)
    usage = usage_init
    program = program_init
    for iteration in range(ITERS):
        usage_top = jnp.dot(expression, program.T, precision=highest)
        program_gram = jnp.dot(program, program.T, precision=highest)
        usage = usage * usage_top / jnp.dot(usage, program_gram, precision=highest)
        program_top = jnp.dot(usage.T, expression, precision=highest)
        usage_gram = jnp.dot(usage.T, usage, precision=highest)
        program = program * program_top / jnp.dot(usage_gram, program, precision=highest)
    return usage, program
```

```python
import functools

import jax
import jax.numpy as jnp
from jax import lax
from jax.experimental import pallas as pl
from jax.experimental.pallas import tpu as pltpu
from jax.sharding import PartitionSpec as P

ITERS = 2
VMEM = pl.BlockSpec(memory_space=pltpu.VMEM)
SMEM = pl.BlockSpec(memory_space=pltpu.SMEM)
PARAMS = pltpu.CompilerParams(vmem_limit_bytes=32 * 1024 * 1024)
F32 = jnp.float32
BF16 = jnp.bfloat16


def split(a):
    high = a.astype(BF16)
    return high, (a - high.astype(F32)).astype(BF16)


def dot(a, b, a_dim, b_dim):
    return lax.dot_general(a, b, (((a_dim,), (b_dim,)), ((), ())), preferred_element_type=F32)


def dot3(a, b, a_dim, b_dim):
    ah, al = split(a)
    bh, bl = split(b)
    return dot(ah, bh, a_dim, b_dim) + (dot(al, bh, a_dim, b_dim) + dot(ah, bl, a_dim, b_dim))


def call(body, outs, *args, flops):
    specs = [SMEM if a.dtype == jnp.int32 and a.ndim == 1 else VMEM for a in args]
    shapes = [jax.ShapeDtypeStruct(s, F32) for s in outs]
    moved = sum(a.size * a.dtype.itemsize for a in args) + sum(s.size * 4 for s in shapes)
    return pl.pallas_call(
        body,
        out_shape=shapes,
        in_specs=specs,
        out_specs=[VMEM] * len(outs),
        compiler_params=PARAMS,
        cost_estimate=pl.CostEstimate(flops=flops, bytes_accessed=moved, transcendentals=0),
    )(*args)


def gram_rows(a, start, rows):
    def body(start_ref, a_ref, g_ref):
        part = a_ref[pl.ds(pl.multiple_of(start_ref[0], 8), rows), :]
        g_ref[...] = dot3(part, a_ref[...], 1, 1)

    k, n = a.shape
    return call(body, [(rows, k)], start, a, flops=6 * rows * k * n)[0]


def usage_top(program, x, start, rows):
    def body(start_ref, p_ref, x_ref, t_ref):
        ph, plo = split(p_ref[...])
        part = x_ref[pl.ds(pl.multiple_of(start_ref[0], 16), rows), :]
        t_ref[...] = dot(ph, part, 1, 1) + dot(plo, part, 1, 1)

    k, n = program.shape
    return call(body, [(k, rows)], start, program, x, flops=4 * rows * k * n)[0]


def usage_update(gram, usage, top_a, top_b):
    def body(g_ref, u_ref, a_ref, b_ref, o_ref):
        u = u_ref[...]
        o_ref[...] = u * (a_ref[...] + b_ref[...]) / dot3(g_ref[...], u, 1, 0)

    k, n = usage.shape
    return call(body, [(k, n)], gram, usage, top_a, top_b, flops=6 * k * k * n)[0]


def program_top(usage, x, start, column, columns):
    def body(start_ref, column_ref, u_ref, x_ref, t_ref):
        uh, ul = split(u_ref[...])
        rows = pl.ds(pl.multiple_of(start_ref[0], 16), u_ref.shape[1])
        part = x_ref[rows, pl.ds(pl.multiple_of(column_ref[0], 128), columns)]
        t_ref[...] = dot(uh, part, 1, 0) + dot(ul, part, 1, 0)

    if columns % 128:
        x = lax.dynamic_slice_in_dim(x, column[0], columns, 1)
        column = jnp.zeros_like(column)
    k, n = usage.shape
    return call(body, [(k, columns)], start, column, usage, x, flops=4 * k * n * columns)[0]


def exchange(a, axis, size, flip):
    return lax.ppermute(a, axis, [(i, i ^ flip) for i in range(size)])


def body(genes, cells, counts, usage_init, program_init):
    x = counts.astype(BF16)
    cell, gene = lax.axis_index("cell"), lax.axis_index("gene")
    core = cell % 2
    half = (gene ^ (gene >> 1)) % 2
    n_cells, n_genes = counts.shape
    k = program_init.shape[0]
    rows, columns = n_cells // 2, n_genes // 2
    grows = -(-k // 16) * 8
    usage_t = usage_init.T

    def at(index):
        return jnp.full((1,), index, jnp.int32)

    own, other = at(half * rows), at((1 - half) * rows)
    own_col, other_col = at(core * columns), at((1 - core) * columns)
    grow, other_grow = at(core * (k - grows)), at((1 - core) * (k - grows))

    def join(mine, theirs, which, axis):
        first = jnp.where(which == 0, mine, theirs)
        second = jnp.where(which == 0, theirs, mine)
        return first, second, jnp.concatenate([first, second], axis)

    def whole_gram(mine):
        theirs = exchange(mine, "cell", cells, 1)
        first, second, _ = join(mine, theirs, core, 0)
        return jnp.concatenate([first, second[2 * grows - k :]], 0)

    usage = lax.dynamic_slice_in_dim(usage_t, half * rows, rows, 1)
    program = program_init
    program_half = lax.dynamic_slice_in_dim(program_init, core * columns, columns, 1)
    for _ in range(ITERS):
        gram = gram_rows(program, grow, grows)
        send = usage_top(program, x, other, rows)
        gram = gram + exchange(gram, "gene", genes, 1)
        near = exchange(send, "gene", genes, 1)
        keep = usage_top(program, x, own, rows)
        top = keep + near
        step = 2
        while step < genes:
            gram = gram + exchange(gram, "gene", genes, 2 * step - 1)
            step *= 2
        gram = whole_gram(gram)
        step = 2
        while step < genes:
            add = exchange(top, "gene", genes, 2 * step - 1)
            step *= 2
            if step < genes:
                top = top + add
        usage = usage_update(gram, usage, top, add)
        usage_other = exchange(usage, "gene", genes, 1)
        usage_first, usage_second, usage_t = join(usage, usage_other, half, 1)

        zero = at(0)
        send = program_top(usage_t, x, zero, other_col, columns)
        near = exchange(send, "cell", cells, 1)
        gram_send = gram_rows(usage_t, other_grow, grows)
        gram_near = exchange(gram_send, "cell", cells, 1)
        gram_keep = gram_rows(usage_t, grow, grows)
        keep = program_top(usage_t, x, zero, own_col, columns)
        top = keep + near
        gram = gram_keep + gram_near
        step = 2
        while step < cells:
            gram = gram + exchange(gram, "cell", cells, step)
            step *= 2
        gram = whole_gram(gram)
        step = 2
        while step < cells:
            add = exchange(top, "cell", cells, step)
            step *= 2
            if step < cells:
                top = top + add
        program_half = usage_update(gram, program_half, top, add)
        program_other = exchange(program_half, "cell", cells, 1)
        _, _, program = join(program_half, program_other, core, 1)
    return usage_t.T, program


def solution(mesh):
    return jax.shard_map(
        functools.partial(body, mesh.shape["gene"], mesh.shape["cell"]),
        mesh=mesh,
        in_specs=(P("cell", "gene"), P(("rep", "cell"), None), P("rep", "gene")),
        out_specs=(P(("rep", "cell"), None), P("rep", "gene")),
        check_vma=False,
    )
```

```python
import functools

import jax
import jax.numpy as jnp
from jax import lax
from jax.experimental import pallas as pl
from jax.experimental.pallas import tpu as pltpu
from jax.sharding import PartitionSpec as P

ITERS = 2
VMEM = pl.BlockSpec(memory_space=pltpu.VMEM)
SMEM = pl.BlockSpec(memory_space=pltpu.SMEM)
PARAMS = pltpu.CompilerParams(vmem_limit_bytes=12 * 1024 * 1024)
F32 = jnp.float32
BF16 = jnp.bfloat16


def split(a):
    high = a.astype(BF16)
    return high, (a - high.astype(F32)).astype(BF16)


def dot(a, b, a_dim, b_dim):
    return lax.dot_general(a, b, (((a_dim,), (b_dim,)), ((), ())), preferred_element_type=F32)


def dot3(a, b, a_dim, b_dim):
    ah, al = split(a)
    bh, bl = split(b)
    return dot(ah, bh, a_dim, b_dim) + (dot(al, bh, a_dim, b_dim) + dot(ah, bl, a_dim, b_dim))


def call(body, outs, *args, flops):
    specs = [SMEM if a.dtype == jnp.int32 and a.ndim == 1 else VMEM for a in args]
    shapes = [jax.ShapeDtypeStruct(s, F32) for s in outs]
    moved = sum(a.size * a.dtype.itemsize for a in args) + sum(s.size * 4 for s in shapes)
    return pl.pallas_call(
        body,
        out_shape=shapes,
        in_specs=specs,
        out_specs=[VMEM] * len(outs),
        compiler_params=PARAMS,
        cost_estimate=pl.CostEstimate(flops=flops, bytes_accessed=moved, transcendentals=0),
    )(*args)


def gram_rows(a, start, rows):
    def body(start_ref, a_ref, g_ref):
        part = a_ref[pl.ds(pl.multiple_of(start_ref[0], 8), rows), :]
        g_ref[...] = dot3(part, a_ref[...], 1, 1)

    k, n = a.shape
    return call(body, [(rows, k)], start, a, flops=6 * rows * k * n)[0]


def usage_top(program, x, start, rows):
    def body(start_ref, p_ref, x_ref, t_ref):
        ph, plo = split(p_ref[...])
        part = x_ref[pl.ds(pl.multiple_of(start_ref[0], 16), rows), :]
        t_ref[...] = dot(ph, part, 1, 1) + dot(plo, part, 1, 1)

    k, n = program.shape
    return call(body, [(k, rows)], start, program, x, flops=4 * rows * k * n)[0]


def update(gram, factor, first, rows, top_a, top_b):
    def body(g_ref, u_ref, a_ref, b_ref, o_ref):
        u = u_ref[...]
        part = u_ref[first : first + rows, :]
        o_ref[...] = part * (a_ref[...] + b_ref[...]) / dot3(g_ref[first : first + rows, :], u, 1, 0)

    k, n = factor.shape
    return call(body, [(rows, n)], gram, factor, top_a, top_b, flops=6 * rows * k * n)[0]


def program_top(usage, x, start, column, columns):
    def body(start_ref, column_ref, u_ref, x_ref, t_ref):
        uh, ul = split(u_ref[...])
        rows = pl.ds(pl.multiple_of(start_ref[0], 16), u_ref.shape[1])
        part = x_ref[rows, pl.ds(pl.multiple_of(column_ref[0], 128), columns)]
        t_ref[...] = dot(uh, part, 1, 0) + dot(ul, part, 1, 0)

    if columns % 128:
        x = lax.dynamic_slice_in_dim(x, column[0], columns, 1)
        column = jnp.zeros_like(column)
    k, n = usage.shape
    return call(body, [(k, columns)], start, column, usage, x, flops=4 * k * n * columns)[0]


def exchange(a, axis, size, flip):
    return lax.ppermute(a, axis, [(i, i ^ flip) for i in range(size)])


def body(genes, cells, counts, usage_init, program_init):
    cell, gene = lax.axis_index("cell"), lax.axis_index("gene")
    core = cell % 2
    half = (gene ^ (gene >> 1)) % 2
    n_cells, n_genes = counts.shape
    k = program_init.shape[0]
    rows, columns = n_cells // 2, n_genes // 2
    grows = -(-k // 16) * 8
    chunks = [(0, grows), (grows, k - grows)]

    def at(index):
        return jnp.full((1,), index, jnp.int32)

    own, other = at(half * rows), at((1 - half) * rows)
    own_col, other_col = at(core * columns), at((1 - core) * columns)
    grow, other_grow = at(core * (k - grows)), at((1 - core) * (k - grows))
    zero = at(0)

    def join(mine, theirs, which, axis):
        first = jnp.where(which == 0, mine, theirs)
        second = jnp.where(which == 0, theirs, mine)
        return jnp.concatenate([first, second], axis)

    def whole_gram(mine):
        theirs = exchange(mine, "cell", cells, 1)
        first = jnp.where(core == 0, mine, theirs)
        second = jnp.where(core == 0, theirs, mine)
        return jnp.concatenate([first, second[2 * grows - k :]], 0)

    def far(a, axis, size, mirrored):
        step = 2
        add = jnp.zeros_like(a)
        while step < size:
            if step > 2:
                a = a + add
            add = exchange(a, axis, size, 2 * step - 1 if mirrored else step)
            step *= 2
        return a, add

    x = counts.astype(BF16)
    program = program_init
    parts = [program_init[f : f + n] for f, n in chunks]
    usage_half = lax.dynamic_slice_in_dim(usage_init.T, half * rows, rows, 1)
    program_half = lax.dynamic_slice_in_dim(program_init, core * columns, columns, 1)
    for _ in range(ITERS):
        gram = gram_rows(program, grow, grows)
        gram = gram + exchange(gram, "gene", genes, 1)
        gram, add = far(gram, "gene", genes, True)
        gram = whole_gram(gram + add)
        tops = []
        for part in parts:
            near = exchange(usage_top(part, x, other, rows), "gene", genes, 1)
            tops.append(far(usage_top(part, x, own, rows) + near, "gene", genes, True))
        new = [update(gram, usage_half, f, n, *top) for (f, n), top in zip(chunks, tops)]
        usage_half = jnp.concatenate(new, 0)
        usages = [join(part, exchange(part, "gene", genes, 1), half, 1) for part in new]
        usage = jnp.concatenate(usages, 0)

        gram_near = exchange(gram_rows(usage, other_grow, grows), "cell", cells, 1)
        gram, add = far(gram_rows(usage, grow, grows) + gram_near, "cell", cells, False)
        gram = whole_gram(gram + add)
        tops = []
        for part in usages:
            near = exchange(program_top(part, x, zero, other_col, columns), "cell", cells, 1)
            tops.append(far(program_top(part, x, zero, own_col, columns) + near, "cell", cells, False))
        new = [update(gram, program_half, f, n, *top) for (f, n), top in zip(chunks, tops)]
        program_half = jnp.concatenate(new, 0)
        parts = [join(part, exchange(part, "cell", cells, 1), core, 1) for part in new]
        program = jnp.concatenate(parts, 0)
    return usage.T, program


def solution(mesh):
    return jax.shard_map(
        functools.partial(body, mesh.shape["gene"], mesh.shape["cell"]),
        mesh=mesh,
        in_specs=(P("cell", "gene"), P(("rep", "cell"), None), P("rep", "gene")),
        out_specs=(P(("rep", "cell"), None), P("rep", "gene")),
        check_vma=False,
    )
```

```python
import functools

import jax
import jax.numpy as jnp
from jax import lax
from jax.experimental import pallas as pl
from jax.experimental.pallas import tpu as pltpu
from jax.sharding import PartitionSpec as P

ITERS = 2
FIRST_ROWS = 104
GRAM_AT = 1
WEIGHT = 12
VMEM = pl.BlockSpec(memory_space=pltpu.VMEM)
SMEM = pl.BlockSpec(memory_space=pltpu.SMEM)
ANY = pl.BlockSpec(memory_space=pl.ANY)
HBM = pl.BlockSpec(memory_space=pltpu.HBM)
PARAMS = pltpu.CompilerParams(vmem_limit_bytes=16 * 1024 * 1024)
F32 = jnp.float32
BF16 = jnp.bfloat16


def split(a):
    high = a.astype(BF16)
    return high, (a - high.astype(F32)).astype(BF16)


def dot(a, b, a_dim, b_dim):
    return lax.dot_general(a, b, (((a_dim,), (b_dim,)), ((), ())), preferred_element_type=F32)


def dot2(a, b, a_dim, b_dim):
    high, low = split(a)
    return dot(high, b, a_dim, b_dim) + dot(low, b, a_dim, b_dim)


def dot3(a, b, a_dim, b_dim):
    ah, al = split(a)
    bh, bl = split(b)
    return dot(ah, bh, a_dim, b_dim) + (dot(al, bh, a_dim, b_dim) + dot(ah, bl, a_dim, b_dim))


class Chain:
    def __init__(self):
        self.last = None

    def __call__(self, body, outs, *args, flops=0, any_args=(), scratch=()):
        specs = [
            SMEM if a.dtype == jnp.int32 and a.ndim == 1 else HBM if i in any_args else VMEM
            for i, a in enumerate(args)
        ]
        shapes = [s if isinstance(s, jax.ShapeDtypeStruct) else jax.ShapeDtypeStruct(s, F32) for s in outs]
        moved = sum(a.size * a.dtype.itemsize for a in args) + sum(s.size * 4 for s in shapes)
        tail = [] if self.last is None else [self.last]
        n_args = len(args)

        def run(*refs):
            body(*refs[:n_args], *refs[n_args + len(tail) :])

        result = pl.pallas_call(
            run,
            out_shape=[pltpu.VMEM(s.shape, s.dtype) for s in shapes],
            in_specs=specs + [ANY] * len(tail),
            out_specs=[VMEM] * len(outs),
            scratch_shapes=scratch,
            compiler_params=PARAMS,
            cost_estimate=pl.CostEstimate(flops=flops, bytes_accessed=moved, transcendentals=0),
        )(*args, *tail)
        self.last = result[0]
        return result


def exchange(a, axis, size, flip):
    return lax.ppermute(a, axis, [(i, i ^ flip) for i in range(size)])


def body(genes, cells, counts, usage_init, program_init):
    cell, gene = lax.axis_index("cell"), lax.axis_index("gene")
    core = cell % 2
    half = (gene ^ (gene >> 1)) % 2
    n_cells, n_genes = counts.shape
    k = program_init.shape[0]
    rows, columns = n_cells // 2, n_genes // 2
    grows = -(-k // 16) * 8
    first_size = FIRST_ROWS if k > FIRST_ROWS else grows
    sizes = [first_size, k - first_size]
    where = jnp.stack([core, half]).astype(jnp.int32)
    chain = Chain()

    def stacked(refs):
        return jnp.concatenate([r[...] for r in refs], 0)

    def whole_gram(parts):
        return sum(dot3(a, a, 1, 1) for a in parts)

    def share(g, first):
        return jnp.where(first, g[:grows], g[k - grows :])

    def gram(factor_a, factor_b, both):
        def kernel(where_ref, a0, a1, b0, b1, *outs):
            g = whole_gram([stacked((a0, a1)), stacked((b0, b1))])
            first = where_ref[0] == 0
            if both:
                outs[0][...] = share(g, jnp.logical_not(first))
            outs[-1][...] = share(g, first)

        n = factor_a[0].shape[1] + factor_b[0].shape[1]
        return chain(kernel, [(grows, k)] * (1 + both), where, *factor_a, *factor_b, flops=6 * k * k * n)

    def product(a, b, xa, xb, dim):
        parts = len(a)

        def kernel(*refs):
            a_refs, b_refs, (xa_ref, xb_ref, o_ref) = refs[:parts], refs[parts : 2 * parts], refs[2 * parts :]
            o_ref[...] = dot2(stacked(a_refs), xa_ref[...], 1, dim) + dot2(stacked(b_refs), xb_ref[...], 1, dim)

        n, m = sum(r.shape[0] for r in a), xa.shape[1 - dim]
        return chain(kernel, [(n, m)], *a, *b, xa, xb, flops=8 * n * a[0].shape[1] * m)[0]

    def add(a, b):
        def kernel(a_ref, b_ref, o_ref):
            o_ref[...] = a_ref[...] + b_ref[...]

        return chain(kernel, [a.shape], a, b)[0]

    def update(index, mine, theirs, factor, tops, weight=1):
        first = index * sizes[0]

        def rows_of(a):
            return a if a.shape[0] == sizes[index] else a[first : first + sizes[index]]

        def kernel(where_ref, m_ref, t_ref, f0, f1, *refs):
            *top_refs, o_ref = refs
            own = where_ref[0] == 0
            upper = jnp.where(own, m_ref[...], t_ref[...])
            lower = jnp.where(own, t_ref[...], m_ref[...])
            g = rows_of(jnp.concatenate([upper, lower[2 * grows - k :]], 0))
            f = stacked((f0, f1))
            part = (f0, f1)[index][...]
            top = sum(rows_of(ref[...]) for ref in top_refs)
            o_ref[...] = part * top / dot3(g, f, 1, 0)

        n, m = factor[index].shape
        return chain(kernel, [(n, m)], where, mine, theirs, *factor, *tops, flops=6 * n * k * m * weight)[0]

    def far(a, axis, size, mirrored):
        step = 2
        other = jnp.zeros_like(a)
        while step < size:
            if step > 2:
                a = a + other
            other = exchange(a, axis, size, 2 * step - 1 if mirrored else step)
            step *= 2
        return a, other

    if columns % 128 == 0 and rows % 32 == 0:
        pieces = 4
        piece = rows // pieces

        def halves(a, which, size):
            first, second = a[:, :size], a[:, size:]
            return jnp.where(which, second, first), jnp.where(which, first, second)

        def load(start, counts_ref, buffer, sems):
            copies = [
                pltpu.make_async_copy(
                    counts_ref.at[pl.ds(pl.multiple_of(start + i * piece, 8), piece)], buffer.at[i], sems.at[i]
                )
                for i in range(pieces)
            ]
            for copy in copies:
                copy.start()
            return copies

        def convert(copies, swap, x_refs, buffer):
            for i, copy in enumerate(copies):
                copy.wait()
                at = slice(i * piece, (i + 1) * piece)
                own, other = halves(buffer[i].astype(F32), swap, columns)
                x_refs[0][at, :], x_refs[1][at, :] = own.astype(BF16), other.astype(BF16)

        def prepare(where_ref, p_ref, counts_ref, g_ref, s0, s1, a0, a1, b0, b1, x0, x1, p, buffer, p_sem, sems):
            copy = pltpu.make_async_copy(p_ref, p, p_sem)
            copy.start()
            copies = load((1 - where_ref[1]) * rows, counts_ref, buffer, sems)
            copy.wait()
            own, other = halves(p[...], where_ref[0] == 1, columns)
            for part, refs in ((own, (a0, a1)), (other, (b0, b1))):
                refs[0][...], refs[1][...] = part[: sizes[0]], part[sizes[0] :]
            g_ref[...] = share(whole_gram([own, other]), where_ref[0] == 0)
            convert(copies, where_ref[0] == 1, (x0, x1), buffer)
            s = dot2(own, x0[...], 1, 1) + dot2(other, x1[...], 1, 1)
            s0[...], s1[...] = s[: sizes[0]], s[sizes[0] :]

        def load_own(where_ref, counts_ref, a0, a1, b0, b1, u_ref, k0, k1, x0, x1, u0, u1, buffer, sems):
            copies = load(where_ref[1] * rows, counts_ref, buffer, sems)
            mine, _ = halves(u_ref[...], where_ref[1] == 1, rows)
            u0[...], u1[...] = mine[: sizes[0]], mine[sizes[0] :]
            convert(copies, where_ref[0] == 1, (x0, x1), buffer)
            keep = dot2(stacked((a0, a1)), x0[...], 1, 1) + dot2(stacked((b0, b1)), x1[...], 1, 1)
            k0[...], k1[...] = keep[: sizes[0]], keep[sizes[0] :]

        half_x = [jax.ShapeDtypeStruct((rows, columns), BF16)] * 2
        buffer = pltpu.VMEM((pieces, piece, n_genes), jnp.int32)
        sems = pltpu.SemaphoreType.DMA((pieces,))
        flops = 4 * k * rows * n_genes
        gram_p, s0, s1, *rest = chain(
            prepare,
            [(grows, k)] + [(n, rows) for n in sizes] + [(n, columns) for n in sizes] * 2 + half_x,
            where,
            program_init,
            pltpu.with_memory_space_constraint(counts, pltpu.HBM),
            flops=flops,
            any_args=(1, 2),
            scratch=[pltpu.VMEM(program_init.shape, F32), buffer, pltpu.SemaphoreType.DMA, sems],
        )
        program_own, program_other, x_other = list(rest[:2]), list(rest[2:4]), list(rest[4:])
        gram_near = exchange(gram_p, "gene", genes, 1)
        nears = [exchange(a, "gene", genes, 1) for a in (s0, s1)]
        keep0, keep1, x0, x1, u0, u1 = chain(
            load_own,
            [(n, rows) for n in sizes] + half_x + [(n, rows) for n in sizes],
            where,
            pltpu.with_memory_space_constraint(counts, pltpu.HBM),
            *program_own,
            *program_other,
            usage_init.T,
            flops=flops,
            any_args=(1,),
            scratch=[buffer, sems],
        )
        x = [[x0, x1], x_other]
        usage_own = [u0, u1]
        keeps = [keep0, keep1]
    else:

        def at(a, which, axis):
            size = a.shape[axis] // 2
            return [lax.dynamic_slice_in_dim(a, i * size, size, axis) for i in (which, 1 - which)]

        def chunked(a):
            return [a[:first_size], a[first_size:]]

        x = [at(part, core, 1) for part in at(counts.astype(BF16), half, 0)]
        program_own, program_other = [chunked(a) for a in at(program_init, core, 1)]
        usage_own = chunked(at(usage_init.T, half, 1)[0])
        gram_p = gram(program_own, program_other, False)[0]
        gram_near = exchange(gram_p, "gene", genes, 1)
        nears, keeps = [], []
        for i in range(2):
            a, b = program_own[i : i + 1], program_other[i : i + 1]
            nears.append(exchange(product(a, b, *x[1], 1), "gene", genes, 1))
            keeps.append(product(a, b, *x[0], 1))

    for iteration in range(ITERS):
        if iteration:
            nears, keeps = [], []
            for i in range(2):
                a, b = program_own[i : i + 1], program_other[i : i + 1]
                if i == GRAM_AT:
                    gram_p = gram(program_own, program_other, False)[0]
                    gram_near = exchange(gram_p, "gene", genes, 1)
                nears.append(exchange(product(a, b, *x[1], 1), "gene", genes, 1))
                keeps.append(product(a, b, *x[0], 1))
        gram_top = far(add(gram_p, gram_near), "gene", genes, True)
        tops = [far(add(keep, near), "gene", genes, True) for keep, near in zip(keeps, nears)]
        mine = add(*gram_top)
        theirs = exchange(mine, "cell", cells, 1)
        new, other = [], []
        for i in range(2):
            new.append(update(i, mine, theirs, usage_own, tops[i], weight=WEIGHT if i else 1))
            other.append(exchange(new[i], "gene", genes, 1))
        usage_own, usage_other = new, other

        sends = [exchange(product(new[:1], other[:1], x[0][1], x[1][1], 0), "cell", cells, 1)]
        keeps = [product(new[:1], other[:1], x[0][0], x[1][0], 0)]
        tops = [far(add(keeps[0], sends[0]), "cell", cells, False)]
        gram_send, gram_keep = gram(usage_own, usage_other, True)
        gram_near = exchange(gram_send, "cell", cells, 1)
        send = product(new[1:], other[1:], x[0][1], x[1][1], 0)
        sends.append(exchange(send, "cell", cells, 1))
        keeps.append(product(new[1:], other[1:], x[0][0], x[1][0], 0))
        tops[0] = (add(*tops[0]),)
        gram_top = far(add(gram_keep, gram_near), "cell", cells, False)
        tops.append(far(add(keeps[1], sends[1]), "cell", cells, False))
        mine = add(*gram_top)
        theirs = exchange(mine, "cell", cells, 1)
        new, other = [], []
        for i in range(2):
            new.append(update(i, mine, theirs, program_own, tops[i]))
            other.append(exchange(new[i], "cell", cells, 1))
        program_own, program_other = new, other

    def join(mine, theirs, which):
        mine, theirs = jnp.concatenate(mine, 0), jnp.concatenate(theirs, 0)
        return jnp.concatenate([jnp.where(which == 0, mine, theirs), jnp.where(which == 0, theirs, mine)], 1)

    return join(usage_own, usage_other, half).T, join(program_own, program_other, core)


def solution(mesh):
    return jax.shard_map(
        functools.partial(body, mesh.shape["gene"], mesh.shape["cell"]),
        mesh=mesh,
        in_specs=(P("cell", "gene"), P(("rep", "cell"), None), P("rep", "gene")),
        out_specs=(P(("rep", "cell"), None), P("rep", "gene")),
        check_vma=False,
    )
```

```python
import functools

import jax
import jax.numpy as jnp
from jax import lax
from jax.experimental import pallas as pl
from jax.experimental.pallas import tpu as pltpu
from jax.sharding import PartitionSpec as P

ITERS = 2
FIRST_ROWS = 104
GRAM_AT = 1
WEIGHT = 12
LAST_WEIGHT = 12
VMEM = pl.BlockSpec(memory_space=pltpu.VMEM)
SMEM = pl.BlockSpec(memory_space=pltpu.SMEM)
ANY = pl.BlockSpec(memory_space=pl.ANY)
HBM = pl.BlockSpec(memory_space=pltpu.HBM)
PARAMS = pltpu.CompilerParams(vmem_limit_bytes=16 * 1024 * 1024)
F32 = jnp.float32
BF16 = jnp.bfloat16


def split(a):
    high = a.astype(BF16)
    return high, (a - high.astype(F32)).astype(BF16)


def dot(a, b, a_dim, b_dim):
    return lax.dot_general(a, b, (((a_dim,), (b_dim,)), ((), ())), preferred_element_type=F32)


def dot2(a, b, a_dim, b_dim):
    high, low = split(a)
    return dot(high, b, a_dim, b_dim) + dot(low, b, a_dim, b_dim)


def dot3(a, b, a_dim, b_dim):
    ah, al = split(a)
    bh, bl = split(b)
    return dot(ah, bh, a_dim, b_dim) + (dot(al, bh, a_dim, b_dim) + dot(ah, bl, a_dim, b_dim))


class Chain:
    def __init__(self):
        self.last = None

    def __call__(self, body, outs, *args, flops=0, any_args=(), scratch=()):
        specs = [
            SMEM if a.dtype == jnp.int32 and a.ndim == 1 else HBM if i in any_args else VMEM
            for i, a in enumerate(args)
        ]
        shapes = [s if isinstance(s, jax.ShapeDtypeStruct) else jax.ShapeDtypeStruct(s, F32) for s in outs]
        moved = sum(a.size * a.dtype.itemsize for a in args) + sum(s.size * 4 for s in shapes)
        tail = [] if self.last is None else [self.last]
        n_args = len(args)

        def run(*refs):
            body(*refs[:n_args], *refs[n_args + len(tail) :])

        result = pl.pallas_call(
            run,
            out_shape=[pltpu.VMEM(s.shape, s.dtype) for s in shapes],
            in_specs=specs + [ANY] * len(tail),
            out_specs=[VMEM] * len(outs),
            scratch_shapes=scratch,
            compiler_params=PARAMS,
            cost_estimate=pl.CostEstimate(flops=flops, bytes_accessed=moved, transcendentals=0),
        )(*args, *tail)
        self.last = result[0]
        return result


def exchange(a, axis, size, flip):
    return lax.ppermute(a, axis, [(i, i ^ flip) for i in range(size)])


def body(genes, cells, counts, usage_init, program_init):
    cell, gene = lax.axis_index("cell"), lax.axis_index("gene")
    core = cell % 2
    half = (gene ^ (gene >> 1)) % 2
    n_cells, n_genes = counts.shape
    k = program_init.shape[0]
    rows, columns = n_cells // 2, n_genes // 2
    grows = -(-k // 16) * 8
    first_size = FIRST_ROWS if k > FIRST_ROWS else grows
    sizes = [first_size, k - first_size]
    where = jnp.stack([core, half]).astype(jnp.int32)
    chain = Chain()

    def stacked(refs):
        return jnp.concatenate([r[...] for r in refs], 0)

    def whole_gram(parts):
        return sum(dot3(a, a, 1, 1) for a in parts)

    def share(g, first):
        return jnp.where(first, g[:grows], g[k - grows :])

    def gram(factor_a, factor_b, both):
        def kernel(where_ref, a0, a1, b0, b1, *outs):
            g = whole_gram([stacked((a0, a1)), stacked((b0, b1))])
            first = where_ref[0] == 0
            if both:
                outs[0][...] = share(g, jnp.logical_not(first))
            outs[-1][...] = share(g, first)

        n = factor_a[0].shape[1] + factor_b[0].shape[1]
        return chain(kernel, [(grows, k)] * (1 + both), where, *factor_a, *factor_b, flops=6 * k * k * n)

    def product(a, b, xa, xb, dim, cut=0):
        parts = len(a)

        def kernel(*refs):
            a_refs, b_refs, (xa_ref, xb_ref, *o_refs) = refs[:parts], refs[parts : 2 * parts], refs[2 * parts :]
            o = dot2(stacked(a_refs), xa_ref[...], 1, dim) + dot2(stacked(b_refs), xb_ref[...], 1, dim)
            if cut:
                o_refs[0][...], o_refs[1][...] = o[:cut], o[cut:]
            else:
                o_refs[0][...] = o

        n, m = sum(r.shape[0] for r in a), xa.shape[1 - dim]
        outs = [(cut, m), (n - cut, m)] if cut else [(n, m)]
        result = chain(kernel, outs, *a, *b, xa, xb, flops=8 * n * a[0].shape[1] * m)
        return result if cut else result[0]

    def add(a, *b):
        def kernel(a_ref, *refs):
            *b_refs, o_ref = refs
            o_ref[...] = a_ref[...] + stacked(b_refs)

        return chain(kernel, [a.shape], a, *b)[0]

    def update(index, mine, theirs, factor, tops, weight=1):
        first = index * sizes[0]

        def rows_of(a):
            return a if a.shape[0] == sizes[index] else a[first : first + sizes[index]]

        def kernel(where_ref, m_ref, t_ref, f0, f1, *refs):
            *top_refs, o_ref = refs
            own = where_ref[0] == 0
            upper = jnp.where(own, m_ref[...], t_ref[...])
            lower = jnp.where(own, t_ref[...], m_ref[...])
            g = rows_of(jnp.concatenate([upper, lower[2 * grows - k :]], 0))
            f = stacked((f0, f1))
            part = (f0, f1)[index][...]
            top = sum(rows_of(ref[...]) for ref in top_refs)
            o_ref[...] = part * top / dot3(g, f, 1, 0)

        n, m = factor[index].shape
        return chain(kernel, [(n, m)], where, mine, theirs, *factor, *tops, flops=6 * n * k * m * weight)[0]

    def join(mine, theirs, index, which):
        size = mine[0].shape[1]
        if size % 128:
            mine, theirs = jnp.concatenate(mine, 0), jnp.concatenate(theirs, 0)
            return jnp.concatenate([jnp.where(which == 0, mine, theirs), jnp.where(which == 0, theirs, mine)], 1)

        def kernel(where_ref, m0, m1, t0, t1, o_ref):
            first = where_ref[index] == 0
            for a, b, rows_at in ((m0, t0, slice(0, sizes[0])), (m1, t1, slice(sizes[0], k))):
                o_ref[rows_at, :size] = jnp.where(first, a[...], b[...])
                o_ref[rows_at, size:] = jnp.where(first, b[...], a[...])

        return chain(kernel, [(k, 2 * size)], where, *mine, *theirs)[0]

    def far(a, axis, size, mirrored):
        step = 2
        other = jnp.zeros_like(a)
        while step < size:
            if step > 2:
                a = a + other
            other = exchange(a, axis, size, 2 * step - 1 if mirrored else step)
            step *= 2
        return a, other

    if columns % 128 == 0 and rows % 32 == 0:
        pieces = 4
        piece = rows // pieces

        def halves(a, which, size):
            first, second = a[:, :size], a[:, size:]
            return jnp.where(which, second, first), jnp.where(which, first, second)

        def load(start, counts_ref, buffer, sems):
            copies = [
                pltpu.make_async_copy(
                    counts_ref.at[pl.ds(pl.multiple_of(start + i * piece, 8), piece)], buffer.at[i], sems.at[i]
                )
                for i in range(pieces)
            ]
            for copy in copies:
                copy.start()
            return copies

        def convert(copies, swap, x_refs, buffer):
            for i, copy in enumerate(copies):
                copy.wait()
                at = slice(i * piece, (i + 1) * piece)
                own, other = halves(buffer[i].astype(F32), swap, columns)
                x_refs[0][at, :], x_refs[1][at, :] = own.astype(BF16), other.astype(BF16)

        def prepare(where_ref, p_ref, counts_ref, g_ref, s0, s1, a0, a1, b0, b1, x0, x1, p, buffer, p_sem, sems):
            copy = pltpu.make_async_copy(p_ref, p, p_sem)
            copy.start()
            copies = load((1 - where_ref[1]) * rows, counts_ref, buffer, sems)
            copy.wait()
            own, other = halves(p[...], where_ref[0] == 1, columns)
            for part, refs in ((own, (a0, a1)), (other, (b0, b1))):
                refs[0][...], refs[1][...] = part[: sizes[0]], part[sizes[0] :]
            g_ref[...] = share(whole_gram([own, other]), where_ref[0] == 0)
            convert(copies, where_ref[0] == 1, (x0, x1), buffer)
            s = dot2(own, x0[...], 1, 1) + dot2(other, x1[...], 1, 1)
            s0[...], s1[...] = s[: sizes[0]], s[sizes[0] :]

        def load_own(where_ref, counts_ref, a0, a1, b0, b1, u_ref, k0, k1, x0, x1, u0, u1, buffer, sems):
            copies = load(where_ref[1] * rows, counts_ref, buffer, sems)
            mine, _ = halves(u_ref[...], where_ref[1] == 1, rows)
            u0[...], u1[...] = mine[: sizes[0]], mine[sizes[0] :]
            convert(copies, where_ref[0] == 1, (x0, x1), buffer)
            keep = dot2(stacked((a0, a1)), x0[...], 1, 1) + dot2(stacked((b0, b1)), x1[...], 1, 1)
            k0[...], k1[...] = keep[: sizes[0]], keep[sizes[0] :]

        half_x = [jax.ShapeDtypeStruct((rows, columns), BF16)] * 2
        buffer = pltpu.VMEM((pieces, piece, n_genes), jnp.int32)
        sems = pltpu.SemaphoreType.DMA((pieces,))
        flops = 4 * k * rows * n_genes
        gram_p, s0, s1, *rest = chain(
            prepare,
            [(grows, k)] + [(n, rows) for n in sizes] + [(n, columns) for n in sizes] * 2 + half_x,
            where,
            program_init,
            pltpu.with_memory_space_constraint(counts, pltpu.HBM),
            flops=flops,
            any_args=(1, 2),
            scratch=[pltpu.VMEM(program_init.shape, F32), buffer, pltpu.SemaphoreType.DMA, sems],
        )
        program_own, program_other, x_other = list(rest[:2]), list(rest[2:4]), list(rest[4:])
        gram_near = exchange(gram_p, "gene", genes, 1)
        nears = [exchange(a, "gene", genes, 1) for a in (s0, s1)]
        keep0, keep1, x0, x1, u0, u1 = chain(
            load_own,
            [(n, rows) for n in sizes] + half_x + [(n, rows) for n in sizes],
            where,
            pltpu.with_memory_space_constraint(counts, pltpu.HBM),
            *program_own,
            *program_other,
            usage_init.T,
            flops=flops,
            any_args=(1,),
            scratch=[buffer, sems],
        )
        x = [[x0, x1], x_other]
        usage_own = [u0, u1]
        keeps = [keep0, keep1]
    else:

        def at(a, which, axis):
            size = a.shape[axis] // 2
            return [lax.dynamic_slice_in_dim(a, i * size, size, axis) for i in (which, 1 - which)]

        def chunked(a):
            return [a[:first_size], a[first_size:]]

        x = [at(part, core, 1) for part in at(counts.astype(BF16), half, 0)]
        program_own, program_other = [chunked(a) for a in at(program_init, core, 1)]
        usage_own = chunked(at(usage_init.T, half, 1)[0])
        gram_p = gram(program_own, program_other, False)[0]
        gram_near = exchange(gram_p, "gene", genes, 1)
        nears, keeps = [], []
        for i in range(2):
            a, b = program_own[i : i + 1], program_other[i : i + 1]
            nears.append(exchange(product(a, b, *x[1], 1), "gene", genes, 1))
            keeps.append(product(a, b, *x[0], 1))

    for iteration in range(ITERS):
        if iteration:
            nears, keeps = [], []
            for i in range(2):
                a, b = program_own[i : i + 1], program_other[i : i + 1]
                if i == GRAM_AT:
                    gram_p = gram(program_own, program_other, False)[0]
                    gram_near = exchange(gram_p, "gene", genes, 1)
                nears.append(exchange(product(a, b, *x[1], 1), "gene", genes, 1))
                keeps.append(product(a, b, *x[0], 1))
        gram_top = far(add(gram_p, gram_near), "gene", genes, True)
        tops = [far(add(keep, near), "gene", genes, True) for keep, near in zip(keeps, nears)]
        mine = add(*gram_top)
        theirs = exchange(mine, "cell", cells, 1)
        new, other = [], []
        for i in range(2):
            new.append(update(i, mine, theirs, usage_own, tops[i], weight=WEIGHT if i else 1))
            other.append(exchange(new[i], "gene", genes, 1))
        usage_own, usage_other = new, other

        cut = sizes[0] // 16 * 8
        send = product(new[:1], other[:1], x[0][1], x[1][1], 0, cut)
        sends = [[exchange(a, "cell", cells, 1) for a in send]]
        keeps = [product(new[:1], other[:1], x[0][0], x[1][0], 0)]
        tops = [far(add(keeps[0], *sends[0]), "cell", cells, False)]
        gram_send, gram_keep = gram(usage_own, usage_other, True)
        gram_near = exchange(gram_send, "cell", cells, 1)
        send = product(new[1:], other[1:], x[0][1], x[1][1], 0)
        sends.append(exchange(send, "cell", cells, 1))
        keeps.append(product(new[1:], other[1:], x[0][0], x[1][0], 0))
        if iteration == ITERS - 1:
            usage = join(usage_own, usage_other, 1, half)
        gram_top = far(add(gram_keep, gram_near), "cell", cells, False)
        tops[0] = (add(*tops[0]),)
        tops.append(far(add(keeps[1], sends[1]), "cell", cells, False))
        mine = add(*gram_top)
        theirs = exchange(mine, "cell", cells, 1)
        new, other = [], []
        for i in range(2):
            new.append(update(i, mine, theirs, program_own, tops[i], weight=LAST_WEIGHT if i == 0 and iteration == ITERS - 1 else 1))
            other.append(exchange(new[i], "cell", cells, 1))
        program_own, program_other = new, other

    return usage.T, join(program_own, program_other, 0, core)


def solution(mesh):
    return jax.shard_map(
        functools.partial(body, mesh.shape["gene"], mesh.shape["cell"]),
        mesh=mesh,
        in_specs=(P("cell", "gene"), P(("rep", "cell"), None), P("rep", "gene")),
        out_specs=(P(("rep", "cell"), None), P("rep", "gene")),
        check_vma=False,
    )
```

```python
import functools

import jax
import jax.numpy as jnp
from jax import lax
from jax.experimental import pallas as pl
from jax.experimental.pallas import tpu as pltpu
from jax.sharding import PartitionSpec as P

ITERS = 2
FIRST_ROWS = 104
WEIGHT = 12
LAST_WEIGHT = 12
VMEM = pl.BlockSpec(memory_space=pltpu.VMEM)
SMEM = pl.BlockSpec(memory_space=pltpu.SMEM)
ANY = pl.BlockSpec(memory_space=pl.ANY)
HBM = pl.BlockSpec(memory_space=pltpu.HBM)
PARAMS = pltpu.CompilerParams(vmem_limit_bytes=16 * 1024 * 1024)
F32 = jnp.float32
BF16 = jnp.bfloat16


def split(a):
    high = a.astype(BF16)
    return high, (a - high.astype(F32)).astype(BF16)


def dot(a, b, a_dim, b_dim):
    return lax.dot_general(a, b, (((a_dim,), (b_dim,)), ((), ())), preferred_element_type=F32)


def dot2(a, b, a_dim, b_dim):
    high, low = split(a)
    return dot(high, b, a_dim, b_dim) + dot(low, b, a_dim, b_dim)


def dot3(a, b, a_dim, b_dim):
    ah, al = split(a)
    bh, bl = split(b)
    return dot(ah, bh, a_dim, b_dim) + (dot(al, bh, a_dim, b_dim) + dot(ah, bl, a_dim, b_dim))


class Chain:
    def __init__(self):
        self.last = None

    def __call__(self, body, outs, *args, flops=0, any_args=(), scratch=()):
        specs = [
            SMEM if a.dtype == jnp.int32 and a.ndim == 1 else HBM if i in any_args else VMEM
            for i, a in enumerate(args)
        ]
        shapes = [s if isinstance(s, jax.ShapeDtypeStruct) else jax.ShapeDtypeStruct(s, F32) for s in outs]
        moved = sum(a.size * a.dtype.itemsize for a in args) + sum(s.size * 4 for s in shapes)
        tail = [] if self.last is None else [self.last]
        n_args = len(args)

        def run(*refs):
            body(*refs[:n_args], *refs[n_args + len(tail) :])

        result = pl.pallas_call(
            run,
            out_shape=[pltpu.VMEM(s.shape, s.dtype) for s in shapes],
            in_specs=specs + [ANY] * len(tail),
            out_specs=[VMEM] * len(outs),
            scratch_shapes=scratch,
            compiler_params=PARAMS,
            cost_estimate=pl.CostEstimate(flops=flops, bytes_accessed=moved, transcendentals=0),
        )(*args, *tail)
        self.last = result[0]
        return result


def exchange(a, axis, size, flip):
    return lax.ppermute(a, axis, [(i, i ^ flip) for i in range(size)])


def body(genes, cells, counts, usage_init, program_init):
    cell, gene = lax.axis_index("cell"), lax.axis_index("gene")
    core = cell % 2
    half = (gene ^ (gene >> 1)) % 2
    n_cells, n_genes = counts.shape
    k = program_init.shape[0]
    rows, columns = n_cells // 2, n_genes // 2
    grows = -(-k // 16) * 8
    first_size = FIRST_ROWS if k > FIRST_ROWS else grows
    sizes = [first_size, k - first_size]
    where = jnp.stack([core, half]).astype(jnp.int32)
    chain = Chain()

    def stacked(refs):
        return jnp.concatenate([r[...] for r in refs], 0)

    def whole_gram(parts):
        return sum(dot3(a, a, 1, 1) for a in parts)

    def share(g, first):
        return jnp.where(first, g[:grows], g[k - grows :])

    def gram(factor_a, factor_b, both):
        def kernel(where_ref, a0, a1, b0, b1, *outs):
            g = whole_gram([stacked((a0, a1)), stacked((b0, b1))])
            first = where_ref[0] == 0
            if both:
                outs[0][...] = share(g, jnp.logical_not(first))
            outs[-1][...] = share(g, first)

        n = factor_a[0].shape[1] + factor_b[0].shape[1]
        return chain(kernel, [(grows, k)] * (1 + both), where, *factor_a, *factor_b, flops=6 * k * k * n)

    def product(a, b, xa, xb, dim, cut=0):
        parts = len(a)

        def kernel(*refs):
            a_refs, b_refs, (xa_ref, xb_ref, *o_refs) = refs[:parts], refs[parts : 2 * parts], refs[2 * parts :]
            o = dot2(stacked(a_refs), xa_ref[...], 1, dim) + dot2(stacked(b_refs), xb_ref[...], 1, dim)
            if cut:
                o_refs[0][...], o_refs[1][...] = o[:cut], o[cut:]
            else:
                o_refs[0][...] = o

        n, m = sum(r.shape[0] for r in a), xa.shape[1 - dim]
        outs = [(cut, m), (n - cut, m)] if cut else [(n, m)]
        result = chain(kernel, outs, *a, *b, xa, xb, flops=8 * n * a[0].shape[1] * m)
        return result if cut else result[0]

    def add(a, *b):
        def kernel(a_ref, *refs):
            *b_refs, o_ref = refs
            o_ref[...] = a_ref[...] + stacked(b_refs)

        return chain(kernel, [a.shape], a, *b)[0]

    def update(index, mine, theirs, factor, tops, weight=1):
        first = index * sizes[0]

        def rows_of(a):
            return a if a.shape[0] == sizes[index] else a[first : first + sizes[index]]

        def kernel(where_ref, m_ref, t_ref, f0, f1, *refs):
            *top_refs, o_ref = refs
            own = where_ref[0] == 0
            upper = jnp.where(own, m_ref[...], t_ref[...])
            lower = jnp.where(own, t_ref[...], m_ref[...])
            g = rows_of(jnp.concatenate([upper, lower[2 * grows - k :]], 0))
            f = stacked((f0, f1))
            part = (f0, f1)[index][...]
            top = sum(rows_of(ref[...]) for ref in top_refs)
            o_ref[...] = part * top / dot3(g, f, 1, 0)

        n, m = factor[index].shape
        return chain(kernel, [(n, m)], where, mine, theirs, *factor, *tops, flops=6 * n * k * m * weight)[0]

    def join(mine, theirs, index, which):
        size = mine[0].shape[1]
        if size % 128:
            mine, theirs = jnp.concatenate(mine, 0), jnp.concatenate(theirs, 0)
            return jnp.concatenate([jnp.where(which == 0, mine, theirs), jnp.where(which == 0, theirs, mine)], 1)

        def kernel(where_ref, m0, m1, t0, t1, o_ref):
            first = where_ref[index] == 0
            for a, b, rows_at in ((m0, t0, slice(0, sizes[0])), (m1, t1, slice(sizes[0], k))):
                o_ref[rows_at, :size] = jnp.where(first, a[...], b[...])
                o_ref[rows_at, size:] = jnp.where(first, b[...], a[...])

        return chain(kernel, [(k, 2 * size)], where, *mine, *theirs)[0]

    def far(a, axis, size, mirrored):
        step = 2
        other = jnp.zeros_like(a)
        while step < size:
            if step > 2:
                a = a + other
            other = exchange(a, axis, size, 2 * step - 1 if mirrored else step)
            step *= 2
        return a, other

    if columns % 128 == 0 and rows % 32 == 0:
        pieces = 4
        piece = rows // pieces

        def halves(a, which, size):
            first, second = a[:, :size], a[:, size:]
            return jnp.where(which, second, first), jnp.where(which, first, second)

        def load(start, counts_ref, buffer, sems):
            copies = [
                pltpu.make_async_copy(
                    counts_ref.at[pl.ds(pl.multiple_of(start + i * piece, 8), piece)], buffer.at[i], sems.at[i]
                )
                for i in range(pieces)
            ]
            for copy in copies:
                copy.start()
            return copies

        def convert(copies, swap, x_refs, buffer):
            for i, copy in enumerate(copies):
                copy.wait()
                for x_ref, start in zip(x_refs, (swap * columns, (1 - swap) * columns)):
                    part = buffer[i, :, pl.ds(pl.multiple_of(start, 128), columns)]
                    x_ref[i * piece : (i + 1) * piece, :] = part.astype(F32).astype(BF16)

        def prepare(where_ref, p_ref, counts_ref, g_ref, s0, s1, a0, a1, b0, b1, x0, x1, p, buffer, p_sem, sems):
            copy = pltpu.make_async_copy(p_ref, p, p_sem)
            copy.start()
            copies = load((1 - where_ref[1]) * rows, counts_ref, buffer, sems)
            copy.wait()
            own, other = halves(p[...], where_ref[0] == 1, columns)
            for part, refs in ((own, (a0, a1)), (other, (b0, b1))):
                refs[0][...], refs[1][...] = part[: sizes[0]], part[sizes[0] :]
            g_ref[...] = share(whole_gram([own, other]), where_ref[0] == 0)
            convert(copies, where_ref[0], (x0, x1), buffer)
            s = dot2(own, x0[...], 1, 1) + dot2(other, x1[...], 1, 1)
            s0[...], s1[...] = s[: sizes[0]], s[sizes[0] :]

        def load_own(where_ref, counts_ref, a0, a1, b0, b1, u_ref, k0, k1, x0, x1, u0, u1, buffer, sems):
            copies = load(where_ref[1] * rows, counts_ref, buffer, sems)
            mine, _ = halves(u_ref[...], where_ref[1] == 1, rows)
            u0[...], u1[...] = mine[: sizes[0]], mine[sizes[0] :]
            convert(copies, where_ref[0], (x0, x1), buffer)
            keep = dot2(stacked((a0, a1)), x0[...], 1, 1) + dot2(stacked((b0, b1)), x1[...], 1, 1)
            k0[...], k1[...] = keep[: sizes[0]], keep[sizes[0] :]

        half_x = [jax.ShapeDtypeStruct((rows, columns), BF16)] * 2
        buffer = pltpu.VMEM((pieces, piece, n_genes), jnp.int32)
        sems = pltpu.SemaphoreType.DMA((pieces,))
        flops = 4 * k * rows * n_genes
        gram_p, s0, s1, *rest = chain(
            prepare,
            [(grows, k)] + [(n, rows) for n in sizes] + [(n, columns) for n in sizes] * 2 + half_x,
            where,
            pltpu.with_memory_space_constraint(program_init, pltpu.HBM),
            pltpu.with_memory_space_constraint(counts, pltpu.HBM),
            flops=flops,
            any_args=(1, 2),
            scratch=[pltpu.VMEM(program_init.shape, F32), buffer, pltpu.SemaphoreType.DMA, sems],
        )
        program_own, program_other, x_other = list(rest[:2]), list(rest[2:4]), list(rest[4:])
        gram_near = exchange(gram_p, "gene", genes, 1)
        nears = [exchange(a, "gene", genes, 1) for a in (s0, s1)]
        keep0, keep1, x0, x1, u0, u1 = chain(
            load_own,
            [(n, rows) for n in sizes] + half_x + [(n, rows) for n in sizes],
            where,
            pltpu.with_memory_space_constraint(counts, pltpu.HBM),
            *program_own,
            *program_other,
            usage_init.T,
            flops=flops,
            any_args=(1,),
            scratch=[buffer, sems],
        )
        x = [[x0, x1], x_other]
        usage_own = [u0, u1]
        keeps = [keep0, keep1]
    else:

        def at(a, which, axis):
            size = a.shape[axis] // 2
            return [lax.dynamic_slice_in_dim(a, i * size, size, axis) for i in (which, 1 - which)]

        def chunked(a):
            return [a[:first_size], a[first_size:]]

        x = [at(part, core, 1) for part in at(counts.astype(BF16), half, 0)]
        program_own, program_other = [chunked(a) for a in at(program_init, core, 1)]
        usage_own = chunked(at(usage_init.T, half, 1)[0])
        gram_p = gram(program_own, program_other, False)[0]
        gram_near = exchange(gram_p, "gene", genes, 1)
        nears, keeps = [], []
        for i in range(2):
            a, b = program_own[i : i + 1], program_other[i : i + 1]
            nears.append(exchange(product(a, b, *x[1], 1), "gene", genes, 1))
            keeps.append(product(a, b, *x[0], 1))

    for iteration in range(ITERS):
        if iteration:
            a, b = program_own, program_other
            nears = [exchange(product(a[:1], b[:1], *x[1], 1), "gene", genes, 1)]
            keeps = [product(a[:1], b[:1], *x[0], 1)]
            gram_p = gram(a, b, False)[0]
            gram_near = exchange(gram_p, "gene", genes, 1)
            nears.append(exchange(product(a[1:], b[1:], *x[1], 1), "gene", genes, 1))
            keeps.append(product(a[1:], b[1:], *x[0], 1))
        gram_top = far(add(gram_p, gram_near), "gene", genes, True)
        tops = [far(add(keep, near), "gene", genes, True) for keep, near in zip(keeps, nears)]
        mine = add(*gram_top)
        theirs = exchange(mine, "cell", cells, 1)
        new, other = [], []
        for i in range(2):
            new.append(update(i, mine, theirs, usage_own, tops[i], weight=WEIGHT if i else 1))
            other.append(exchange(new[i], "gene", genes, 1))
        usage_own, usage_other = new, other

        cut = sizes[0] // 16 * 8
        send = product(new[:1], other[:1], x[0][1], x[1][1], 0, cut)
        sends = [[exchange(a, "cell", cells, 1) for a in send]]
        keeps = [product(new[:1], other[:1], x[0][0], x[1][0], 0)]
        tops = [far(add(keeps[0], *sends[0]), "cell", cells, False)]
        gram_send, gram_keep = gram(usage_own, usage_other, True)
        gram_near = exchange(gram_send, "cell", cells, 1)
        send = product(new[1:], other[1:], x[0][1], x[1][1], 0)
        sends.append(exchange(send, "cell", cells, 1))
        keeps.append(product(new[1:], other[1:], x[0][0], x[1][0], 0))
        if iteration == ITERS - 1:
            usage = join(usage_own, usage_other, 1, half)
        gram_top = far(add(gram_keep, gram_near), "cell", cells, False)
        tops[0] = (add(*tops[0]),)
        tops.append(far(add(keeps[1], sends[1]), "cell", cells, False))
        mine = add(*gram_top)
        theirs = exchange(mine, "cell", cells, 1)
        new, other = [], []
        last = iteration == ITERS - 1
        for i in range(2):
            new.append(update(i, mine, theirs, program_own, tops[i], weight=LAST_WEIGHT if last and i == 0 else 1))
            other.append(exchange(new[i], "cell", cells, 1))
        program_own, program_other = new, other

    return usage.T, join(program_own, program_other, 0, core)


def solution(mesh):
    return jax.shard_map(
        functools.partial(body, mesh.shape["gene"], mesh.shape["cell"]),
        mesh=mesh,
        in_specs=(P("cell", "gene"), P(("rep", "cell"), None), P("rep", "gene")),
        out_specs=(P(("rep", "cell"), None), P("rep", "gene")),
        check_vma=False,
    )
```

```python
import functools

import jax
import jax.numpy as jnp
from jax import lax
from jax.experimental import pallas as pl
from jax.experimental.pallas import tpu as pltpu
from jax.sharding import PartitionSpec as P

ITERS = 2
CHUNKS = (104, 96)
USAGE_WEIGHTS = (1, 6, 1)
GRAM_AT = 1
PROGRAM_WEIGHTS = (1, 18)
VMEM = pl.BlockSpec(memory_space=pltpu.VMEM)
SMEM = pl.BlockSpec(memory_space=pltpu.SMEM)
ANY = pl.BlockSpec(memory_space=pl.ANY)
HBM = pl.BlockSpec(memory_space=pltpu.HBM)
PARAMS = pltpu.CompilerParams(vmem_limit_bytes=16 * 1024 * 1024)
F32 = jnp.float32
BF16 = jnp.bfloat16


def split(a):
    high = a.astype(BF16)
    return high, (a - high.astype(F32)).astype(BF16)


def dot(a, b, a_dim, b_dim):
    return lax.dot_general(a, b, (((a_dim,), (b_dim,)), ((), ())), preferred_element_type=F32)


def dot2(a, b, a_dim, b_dim):
    high, low = split(a)
    return dot(high, b, a_dim, b_dim) + dot(low, b, a_dim, b_dim)


def dot3(a, b, a_dim, b_dim):
    ah, al = split(a)
    bh, bl = split(b)
    return dot(ah, bh, a_dim, b_dim) + (dot(al, bh, a_dim, b_dim) + dot(ah, bl, a_dim, b_dim))


class Chain:
    def __init__(self):
        self.last = None

    def __call__(self, body, outs, *args, flops=0, any_args=(), scratch=()):
        specs = [
            SMEM if a.dtype == jnp.int32 and a.ndim == 1 else HBM if i in any_args else VMEM
            for i, a in enumerate(args)
        ]
        shapes = [s if isinstance(s, jax.ShapeDtypeStruct) else jax.ShapeDtypeStruct(s, F32) for s in outs]
        moved = sum(a.size * a.dtype.itemsize for a in args) + sum(s.size * 4 for s in shapes)
        tail = [] if self.last is None else [self.last]
        n_args = len(args)

        def run(*refs):
            body(*refs[:n_args], *refs[n_args + len(tail) :])

        result = pl.pallas_call(
            run,
            out_shape=[pltpu.VMEM(s.shape, s.dtype) for s in shapes],
            in_specs=specs + [ANY] * len(tail),
            out_specs=[VMEM] * len(outs),
            scratch_shapes=scratch,
            compiler_params=PARAMS,
            cost_estimate=pl.CostEstimate(flops=flops, bytes_accessed=moved, transcendentals=0),
        )(*args, *tail)
        self.last = result[0]
        return result


def exchange(a, axis, size, flip):
    return lax.ppermute(a, axis, [(i, i ^ flip) for i in range(size)])


def body(genes, cells, counts, usage_init, program_init):
    cell, gene = lax.axis_index("cell"), lax.axis_index("gene")
    core = cell % 2
    half = (gene ^ (gene >> 1)) % 2
    n_cells, n_genes = counts.shape
    k = program_init.shape[0]
    rows, columns = n_cells // 2, n_genes // 2
    sizes = []
    while sum(sizes) < k:
        sizes.append(min(CHUNKS[len(sizes)] if len(sizes) < len(CHUNKS) else k, k - sum(sizes)))
    n_chunks = len(sizes)
    starts = [sum(sizes[:i]) for i in range(n_chunks)]
    where = jnp.stack([core, half]).astype(jnp.int32)
    chain = Chain()

    def stacked(refs):
        return jnp.concatenate([r[...] for r in refs], 0)

    lane = 128
    packs = lane < k <= 2 * lane and k % 8 == 0
    packed = (2 * k - lane, lane) if packs else (-(-k // 16) * 16, k)
    grows = packed[0] // 2

    def packed_gram(parts):
        g = sum(dot3(a, a, 1, 1) for a in parts)
        if packs:
            corner = jnp.concatenate([g[lane:, lane:], jnp.zeros((k - lane, 2 * lane - k), F32)], 1)
            return jnp.concatenate([g[:, :lane], corner], 0)
        return jnp.concatenate([g, jnp.zeros((packed[0] - k, k), F32)], 0) if packed[0] > k else g

    def unpacked(t):
        if packs:
            upper = t[lane : 2 * lane].T[:, : k - lane]
            right = jnp.concatenate([upper, t[k:, : k - lane]], 0)
            return jnp.concatenate([t[:k], right], 1)
        return t[:k]

    def share(t, first):
        return jnp.where(first, t[:grows], t[grows:])

    def gram(factor_a, factor_b, both):
        def kernel(where_ref, *refs):
            a_refs, b_refs, outs = refs[:n_chunks], refs[n_chunks : 2 * n_chunks], refs[2 * n_chunks :]
            t = packed_gram([stacked(a_refs), stacked(b_refs)])
            first = where_ref[0] == 0
            if both:
                outs[0][...] = share(t, jnp.logical_not(first))
            outs[-1][...] = share(t, first)

        n = factor_a[0].shape[1] + factor_b[0].shape[1]
        return chain(kernel, [(grows, packed[1])] * (1 + both), where, *factor_a, *factor_b, flops=6 * k * k * n)

    def product(a, b, xa, xb, dim, cut=0):
        parts = len(a)

        def kernel(*refs):
            a_refs, b_refs, (xa_ref, xb_ref, *o_refs) = refs[:parts], refs[parts : 2 * parts], refs[2 * parts :]
            o = dot2(stacked(a_refs), xa_ref[...], 1, dim) + dot2(stacked(b_refs), xb_ref[...], 1, dim)
            if cut:
                o_refs[0][...], o_refs[1][...] = o[:cut], o[cut:]
            else:
                o_refs[0][...] = o

        n, m = sum(r.shape[0] for r in a), xa.shape[1 - dim]
        outs = [(cut, m), (n - cut, m)] if cut else [(n, m)]
        result = chain(kernel, outs, *a, *b, xa, xb, flops=8 * n * a[0].shape[1] * m)
        return result if cut else result[0]

    def add(a, *b):
        def kernel(a_ref, *refs):
            *b_refs, o_ref = refs
            o_ref[...] = a_ref[...] + stacked(b_refs)

        return chain(kernel, [a.shape], a, *b)[0]

    def update(index, mine, theirs, factor, tops, weight=1):
        first = starts[index]

        def rows_of(a):
            return a if a.shape[0] == sizes[index] else a[first : first + sizes[index]]

        def kernel(where_ref, m_ref, t_ref, *refs):
            f_refs, (*top_refs, o_ref) = refs[:n_chunks], refs[n_chunks:]
            own = where_ref[0] == 0
            upper = jnp.where(own, m_ref[...], t_ref[...])
            lower = jnp.where(own, t_ref[...], m_ref[...])
            g = rows_of(unpacked(jnp.concatenate([upper, lower], 0)))
            f = stacked(f_refs)
            part = f_refs[index][...]
            top = sum(rows_of(ref[...]) for ref in top_refs)
            o_ref[...] = part * top / dot3(g, f, 1, 0)

        n, m = factor[index].shape
        return chain(kernel, [(n, m)], where, mine, theirs, *factor, *tops, flops=6 * n * k * m * weight)[0]

    def join(mine, theirs, index, which):
        size = mine[0].shape[1]
        if size % 128:
            mine, theirs = jnp.concatenate(mine, 0), jnp.concatenate(theirs, 0)
            return jnp.concatenate([jnp.where(which == 0, mine, theirs), jnp.where(which == 0, theirs, mine)], 1)

        def kernel(where_ref, *refs):
            *refs, o_ref = refs
            first = where_ref[index] == 0
            for a, b, start, n in zip(refs[:n_chunks], refs[n_chunks:], starts, sizes):
                o_ref[start : start + n, :size] = jnp.where(first, a[...], b[...])
                o_ref[start : start + n, size:] = jnp.where(first, b[...], a[...])

        return chain(kernel, [(k, 2 * size)], where, *mine, *theirs)[0]

    def far(a, axis, size, mirrored):
        step = 2
        other = jnp.zeros_like(a)
        while step < size:
            if step > 2:
                a = a + other
            other = exchange(a, axis, size, 2 * step - 1 if mirrored else step)
            step *= 2
        return a, other

    if columns % 128 == 0 and rows % 32 == 0:
        pieces = 4
        piece = rows // pieces

        def halves(a, which, size):
            first, second = a[:, :size], a[:, size:]
            return jnp.where(which, second, first), jnp.where(which, first, second)

        def load(start, counts_ref, buffer, sems):
            copies = [
                pltpu.make_async_copy(
                    counts_ref.at[pl.ds(pl.multiple_of(start + i * piece, 8), piece)], buffer.at[i], sems.at[i]
                )
                for i in range(pieces)
            ]
            for copy in copies:
                copy.start()
            return copies

        def convert(copies, swap, x_refs, buffer):
            for i, copy in enumerate(copies):
                copy.wait()
                for x_ref, start in zip(x_refs, (swap * columns, (1 - swap) * columns)):
                    part = buffer[i, :, pl.ds(pl.multiple_of(start, 128), columns)]
                    x_ref[i * piece : (i + 1) * piece, :] = part.astype(F32).astype(BF16)

        def scatter(a, refs):
            for start, n, ref in zip(starts, sizes, refs):
                ref[...] = a[start : start + n]

        def prepare(where_ref, p_ref, counts_ref, g_ref, *refs):
            s_refs, a_refs, b_refs = [refs[i * n_chunks : (i + 1) * n_chunks] for i in range(3)]
            x0, x1, p, buffer, p_sem, sems = refs[3 * n_chunks :]
            copy = pltpu.make_async_copy(p_ref, p, p_sem)
            copy.start()
            copies = load((1 - where_ref[1]) * rows, counts_ref, buffer, sems)
            copy.wait()
            own, other = halves(p[...], where_ref[0] == 1, columns)
            scatter(own, a_refs)
            scatter(other, b_refs)
            g_ref[...] = share(packed_gram([own, other]), where_ref[0] == 0)
            convert(copies, where_ref[0], (x0, x1), buffer)
            scatter(dot2(own, x0[...], 1, 1) + dot2(other, x1[...], 1, 1), s_refs)

        def load_own(where_ref, counts_ref, *refs):
            a_refs, b_refs = refs[:n_chunks], refs[n_chunks : 2 * n_chunks]
            u_ref, *refs = refs[2 * n_chunks :]
            x0, x1, *refs = refs
            k_refs, u_refs, (buffer, sems) = refs[:n_chunks], refs[n_chunks : 2 * n_chunks], refs[2 * n_chunks :]
            copies = load(where_ref[1] * rows, counts_ref, buffer, sems)
            mine, _ = halves(u_ref[...], where_ref[1] == 1, rows)
            scatter(mine, u_refs)
            convert(copies, where_ref[0], (x0, x1), buffer)
            scatter(dot2(stacked(a_refs), x0[...], 1, 1) + dot2(stacked(b_refs), x1[...], 1, 1), k_refs)

        half_x = [jax.ShapeDtypeStruct((rows, columns), BF16)] * 2
        buffer = pltpu.VMEM((pieces, piece, n_genes), jnp.int32)
        sems = pltpu.SemaphoreType.DMA((pieces,))
        flops = 4 * k * rows * n_genes
        gram_p, *rest = chain(
            prepare,
            [(grows, packed[1])] + [(n, rows) for n in sizes] + [(n, columns) for n in sizes] * 2 + half_x,
            where,
            pltpu.with_memory_space_constraint(program_init, pltpu.HBM),
            pltpu.with_memory_space_constraint(counts, pltpu.HBM),
            flops=flops,
            any_args=(1, 2),
            scratch=[pltpu.VMEM(program_init.shape, F32), buffer, pltpu.SemaphoreType.DMA, sems],
        )
        sends, program_own, program_other = [list(rest[i * n_chunks : (i + 1) * n_chunks]) for i in range(3)]
        x_other = list(rest[3 * n_chunks :])
        gram_near = exchange(gram_p, "gene", genes, 1)
        nears = [exchange(a, "gene", genes, 1) for a in sends]
        x0, x1, *rest = chain(
            load_own,
            half_x + [(n, rows) for n in sizes] * 2,
            where,
            pltpu.with_memory_space_constraint(counts, pltpu.HBM),
            *program_own,
            *program_other,
            usage_init.T,
            flops=flops,
            any_args=(1,),
            scratch=[buffer, sems],
        )
        x = [[x0, x1], x_other]
        keeps, usage_own = rest[:n_chunks], rest[n_chunks:]
    else:

        def at(a, which, axis):
            size = a.shape[axis] // 2
            return [lax.dynamic_slice_in_dim(a, i * size, size, axis) for i in (which, 1 - which)]

        def chunked(a):
            return [a[i : i + n] for i, n in zip(starts, sizes)]

        x = [at(part, core, 1) for part in at(counts.astype(BF16), half, 0)]
        program_own, program_other = [chunked(a) for a in at(program_init, core, 1)]
        usage_own = chunked(at(usage_init.T, half, 1)[0])
        gram_p = gram(program_own, program_other, False)[0]
        gram_near = exchange(gram_p, "gene", genes, 1)
        nears, keeps = [], []
        for i in range(n_chunks):
            a, b = program_own[i : i + 1], program_other[i : i + 1]
            nears.append(exchange(product(a, b, *x[1], 1), "gene", genes, 1))
            keeps.append(product(a, b, *x[0], 1))

    for iteration in range(ITERS):
        last = iteration == ITERS - 1
        if iteration:
            nears, keeps = [], []
            for i in range(n_chunks):
                a, b = program_own[i : i + 1], program_other[i : i + 1]
                if i == GRAM_AT:
                    gram_p = gram(program_own, program_other, False)[0]
                    gram_near = exchange(gram_p, "gene", genes, 1)
                nears.append(exchange(product(a, b, *x[1], 1), "gene", genes, 1))
                keeps.append(product(a, b, *x[0], 1))
        gram_top = far(add(gram_p, gram_near), "gene", genes, True)
        tops = [far(add(keep, near), "gene", genes, True) for keep, near in zip(keeps, nears)]
        mine = add(*gram_top)
        theirs = exchange(mine, "cell", cells, 1)
        new, other = [], []
        for i in range(n_chunks):
            new.append(update(i, mine, theirs, usage_own, tops[i], weight=USAGE_WEIGHTS[min(i, 2)]))
            other.append(exchange(new[i], "gene", genes, 1))
        usage_own, usage_other = new, other

        tops = []
        for i in range(n_chunks):
            a, b = new[i : i + 1], other[i : i + 1]
            if i < n_chunks - 1:
                cut = sizes[i] // 16 * 8
                send = [exchange(part, "cell", cells, 1) for part in product(a, b, x[0][1], x[1][1], 0, cut)]
                keep = product(a, b, x[0][0], x[1][0], 0)
                tops.append(far(add(keep, *send), "cell", cells, False))
                continue
            gram_send, gram_keep = gram(usage_own, usage_other, True)
            gram_near = exchange(gram_send, "cell", cells, 1)
            send = exchange(product(a, b, x[0][1], x[1][1], 0), "cell", cells, 1)
            keep = product(a, b, x[0][0], x[1][0], 0)
            if last:
                usage = join(usage_own, usage_other, 1, half)
            gram_top = far(add(gram_keep, gram_near), "cell", cells, False)
            tops = [(add(*top),) for top in tops]
            tops.append(far(add(keep, send), "cell", cells, False))
        mine = add(*gram_top)
        theirs = exchange(mine, "cell", cells, 1)
        new, other = [], []
        for i in range(n_chunks):
            new.append(update(i, mine, theirs, program_own, tops[i], weight=PROGRAM_WEIGHTS[last] if i == 0 else 1))
            other.append(exchange(new[i], "cell", cells, 1))
        program_own, program_other = new, other

    return usage.T, join(program_own, program_other, 0, core)


def solution(mesh):
    return jax.shard_map(
        functools.partial(body, mesh.shape["gene"], mesh.shape["cell"]),
        mesh=mesh,
        in_specs=(P("cell", "gene"), P(("rep", "cell"), None), P("rep", "gene")),
        out_specs=(P(("rep", "cell"), None), P("rep", "gene")),
        check_vma=False,
    )
```

```python
import functools

import jax
import jax.numpy as jnp
from jax import lax
from jax.experimental import pallas as pl
from jax.experimental.pallas import tpu as pltpu
from jax.sharding import PartitionSpec as P

ITERS = 2
CHUNKS = (104, 96)
USAGE_WEIGHTS = (1, 6, 1)
GRAM_AT = 1
PROGRAM_WEIGHTS = (1, 16)
VMEM = pl.BlockSpec(memory_space=pltpu.VMEM)
SMEM = pl.BlockSpec(memory_space=pltpu.SMEM)
ANY = pl.BlockSpec(memory_space=pl.ANY)
HBM = pl.BlockSpec(memory_space=pltpu.HBM)
PARAMS = pltpu.CompilerParams(vmem_limit_bytes=16 * 1024 * 1024)
F32 = jnp.float32
BF16 = jnp.bfloat16


def split(a):
    high = a.astype(BF16)
    return high, (a - high.astype(F32)).astype(BF16)


def dot(a, b, a_dim, b_dim):
    return lax.dot_general(a, b, (((a_dim,), (b_dim,)), ((), ())), preferred_element_type=F32)


def dot2(a, b, a_dim, b_dim):
    high, low = split(a)
    return dot(high, b, a_dim, b_dim) + dot(low, b, a_dim, b_dim)


def dot3(a, b, a_dim, b_dim):
    ah, al = split(a)
    bh, bl = split(b)
    return dot(ah, bh, a_dim, b_dim) + (dot(al, bh, a_dim, b_dim) + dot(ah, bl, a_dim, b_dim))


class Chain:
    def __init__(self):
        self.last = None

    def __call__(self, body, outs, *args, flops=0, any_args=(), scratch=()):
        specs = [
            SMEM if a.dtype == jnp.int32 and a.ndim == 1 else HBM if i in any_args else VMEM
            for i, a in enumerate(args)
        ]
        shapes = [s if isinstance(s, jax.ShapeDtypeStruct) else jax.ShapeDtypeStruct(s, F32) for s in outs]
        moved = sum(a.size * a.dtype.itemsize for a in args) + sum(s.size * 4 for s in shapes)
        tail = [] if self.last is None else [self.last]
        n_args = len(args)

        def run(*refs):
            body(*refs[:n_args], *refs[n_args + len(tail) :])

        result = pl.pallas_call(
            run,
            out_shape=[pltpu.VMEM(s.shape, s.dtype) for s in shapes],
            in_specs=specs + [ANY] * len(tail),
            out_specs=[VMEM] * len(outs),
            scratch_shapes=scratch,
            compiler_params=PARAMS,
            cost_estimate=pl.CostEstimate(flops=flops, bytes_accessed=moved, transcendentals=0),
        )(*args, *tail)
        self.last = result[0]
        return result


def exchange(a, axis, size, flip):
    return lax.ppermute(a, axis, [(i, i ^ flip) for i in range(size)])


def body(genes, cells, counts, usage_init, program_init):
    cell, gene = lax.axis_index("cell"), lax.axis_index("gene")
    core = cell % 2
    half = (gene ^ (gene >> 1)) % 2
    n_cells, n_genes = counts.shape
    k = program_init.shape[0]
    rows, columns = n_cells // 2, n_genes // 2
    sizes = []
    while sum(sizes) < k:
        sizes.append(min(CHUNKS[len(sizes)] if len(sizes) < len(CHUNKS) else k, k - sum(sizes)))
    n_chunks = len(sizes)
    starts = [sum(sizes[:i]) for i in range(n_chunks)]
    where = jnp.stack([core, half]).astype(jnp.int32)
    chain = Chain()

    def stacked(refs):
        return jnp.concatenate([r[...] for r in refs], 0)

    lane = 128
    packs = lane < k <= 2 * lane and k % 8 == 0
    packed = (2 * k - lane, lane) if packs else (-(-k // 16) * 16, k)
    grows = packed[0] // 2

    def packed_gram(parts):
        g = sum(dot3(a, a, 1, 1) for a in parts)
        if packs:
            corner = jnp.concatenate([g[lane:, lane:], jnp.zeros((k - lane, 2 * lane - k), F32)], 1)
            return jnp.concatenate([g[:, :lane], corner], 0)
        return jnp.concatenate([g, jnp.zeros((packed[0] - k, k), F32)], 0) if packed[0] > k else g

    def unpacked(t):
        if packs:
            upper = t[lane : 2 * lane].T[:, : k - lane]
            right = jnp.concatenate([upper, t[k:, : k - lane]], 0)
            return jnp.concatenate([t[:k], right], 1)
        return t[:k]

    def share(t, first):
        return jnp.where(first, t[:grows], t[grows:])

    def gram(factor_a, factor_b, both):
        def kernel(where_ref, *refs):
            a_refs, b_refs, outs = refs[:n_chunks], refs[n_chunks : 2 * n_chunks], refs[2 * n_chunks :]
            t = packed_gram([stacked(a_refs), stacked(b_refs)])
            first = where_ref[0] == 0
            if both:
                outs[0][...] = share(t, jnp.logical_not(first))
            outs[-1][...] = share(t, first)

        n = factor_a[0].shape[1] + factor_b[0].shape[1]
        return chain(kernel, [(grows, packed[1])] * (1 + both), where, *factor_a, *factor_b, flops=6 * k * k * n)

    def product(a, b, xa, xb, dim, cut=0):
        parts = len(a)

        def kernel(*refs):
            a_refs, b_refs, (xa_ref, xb_ref, *o_refs) = refs[:parts], refs[parts : 2 * parts], refs[2 * parts :]
            o = dot2(stacked(a_refs), xa_ref[...], 1, dim) + dot2(stacked(b_refs), xb_ref[...], 1, dim)
            if cut:
                o_refs[0][...], o_refs[1][...] = o[:cut], o[cut:]
            else:
                o_refs[0][...] = o

        n, m = sum(r.shape[0] for r in a), xa.shape[1 - dim]
        outs = [(cut, m), (n - cut, m)] if cut else [(n, m)]
        result = chain(kernel, outs, *a, *b, xa, xb, flops=8 * n * a[0].shape[1] * m)
        return result if cut else result[0]

    def add(a, *b):
        def kernel(a_ref, *refs):
            *b_refs, o_ref = refs
            o_ref[...] = a_ref[...] + stacked(b_refs)

        return chain(kernel, [a.shape], a, *b)[0]

    def rows_of(a, index):
        return a[starts[index] : starts[index] + sizes[index]]

    def denominator(where_ref, m_ref, t_ref, f_refs, index):
        own = where_ref[0] == 0
        upper = jnp.where(own, m_ref[...], t_ref[...])
        lower = jnp.where(own, t_ref[...], m_ref[...])
        g = unpacked(jnp.concatenate([upper, lower], 0))
        return dot3(rows_of(g, index), stacked(f_refs), 1, 0)

    def update(mine, theirs, factor, tops, axis, size, flip, weights):
        def first(where_ref, m_ref, t_ref, *refs):
            f_refs, (*top_refs, o_ref) = refs[:n_chunks], refs[n_chunks:]
            below = denominator(where_ref, m_ref, t_ref, f_refs, 0)
            o_ref[...] = f_refs[0][...] * sum(ref[...] for ref in top_refs) / below

        def below(index, where_ref, m_ref, t_ref, *refs):
            refs[-1][...] = denominator(where_ref, m_ref, t_ref, refs[:n_chunks], index)

        def rest(f_ref, d_ref, *refs):
            *top_refs, o_ref = refs
            o_ref[...] = f_ref[...] * sum(ref[...] for ref in top_refs) / d_ref[...]

        m = factor[0].shape[1]
        shapes = [(n, m) for n in sizes]
        flops = [6 * n * k * m * weight for n, weight in zip(sizes, weights)]
        new = [chain(first, shapes[:1], where, mine, theirs, *factor, *tops[0], flops=flops[0])[0]]
        other = [exchange(new[0], axis, size, flip)]
        divisors = [
            chain(functools.partial(below, i), shapes[i : i + 1], where, mine, theirs, *factor)[0]
            for i in range(1, n_chunks)
        ]
        for i in range(1, n_chunks):
            new.append(chain(rest, shapes[i : i + 1], factor[i], divisors[i - 1], *tops[i], flops=flops[i])[0])
            other.append(exchange(new[i], axis, size, flip))
        return new, other

    def join(mine, theirs, index, which):
        size = mine[0].shape[1]
        if size % 128:
            mine, theirs = jnp.concatenate(mine, 0), jnp.concatenate(theirs, 0)
            return jnp.concatenate([jnp.where(which == 0, mine, theirs), jnp.where(which == 0, theirs, mine)], 1)

        def kernel(where_ref, *refs):
            *refs, o_ref = refs
            first = where_ref[index] == 0
            for a, b, start, n in zip(refs[:n_chunks], refs[n_chunks:], starts, sizes):
                o_ref[start : start + n, :size] = jnp.where(first, a[...], b[...])
                o_ref[start : start + n, size:] = jnp.where(first, b[...], a[...])

        return chain(kernel, [(k, 2 * size)], where, *mine, *theirs)[0]

    def far(a, axis, size, mirrored):
        step = 2
        other = jnp.zeros_like(a)
        while step < size:
            if step > 2:
                a = a + other
            other = exchange(a, axis, size, 2 * step - 1 if mirrored else step)
            step *= 2
        return a, other

    if columns % 128 == 0 and rows % 32 == 0:
        pieces = 4
        piece = rows // pieces

        def halves(a, which, size):
            first, second = a[:, :size], a[:, size:]
            return jnp.where(which, second, first), jnp.where(which, first, second)

        def load(start, counts_ref, buffer, sems):
            copies = [
                pltpu.make_async_copy(
                    counts_ref.at[pl.ds(pl.multiple_of(start + i * piece, 8), piece)], buffer.at[i], sems.at[i]
                )
                for i in range(pieces)
            ]
            for copy in copies:
                copy.start()
            return copies

        def convert(copies, swap, x_refs, buffer):
            for i, copy in enumerate(copies):
                copy.wait()
                for x_ref, start in zip(x_refs, (swap * columns, (1 - swap) * columns)):
                    part = buffer[i, :, pl.ds(pl.multiple_of(start, 128), columns)]
                    x_ref[i * piece : (i + 1) * piece, :] = part.astype(F32).astype(BF16)

        def scatter(a, refs):
            for start, n, ref in zip(starts, sizes, refs):
                ref[...] = a[start : start + n]

        def prepare(where_ref, p_ref, counts_ref, g_ref, *refs):
            s_refs, a_refs, b_refs = [refs[i * n_chunks : (i + 1) * n_chunks] for i in range(3)]
            x0, x1, p, buffer, p_sem, sems = refs[3 * n_chunks :]
            copy = pltpu.make_async_copy(p_ref, p, p_sem)
            copy.start()
            copies = load((1 - where_ref[1]) * rows, counts_ref, buffer, sems)
            copy.wait()
            own, other = halves(p[...], where_ref[0] == 1, columns)
            scatter(own, a_refs)
            scatter(other, b_refs)
            g_ref[...] = share(packed_gram([own, other]), where_ref[0] == 0)
            convert(copies, where_ref[0], (x0, x1), buffer)
            scatter(dot2(own, x0[...], 1, 1) + dot2(other, x1[...], 1, 1), s_refs)

        def load_own(where_ref, counts_ref, *refs):
            a_refs, b_refs = refs[:n_chunks], refs[n_chunks : 2 * n_chunks]
            u_ref, *refs = refs[2 * n_chunks :]
            x0, x1, *refs = refs
            k_refs, u_refs, (buffer, sems) = refs[:n_chunks], refs[n_chunks : 2 * n_chunks], refs[2 * n_chunks :]
            copies = load(where_ref[1] * rows, counts_ref, buffer, sems)
            mine, _ = halves(u_ref[...], where_ref[1] == 1, rows)
            scatter(mine, u_refs)
            convert(copies, where_ref[0], (x0, x1), buffer)
            scatter(dot2(stacked(a_refs), x0[...], 1, 1) + dot2(stacked(b_refs), x1[...], 1, 1), k_refs)

        half_x = [jax.ShapeDtypeStruct((rows, columns), BF16)] * 2
        buffer = pltpu.VMEM((pieces, piece, n_genes), jnp.int32)
        sems = pltpu.SemaphoreType.DMA((pieces,))
        flops = 4 * k * rows * n_genes
        gram_p, *rest = chain(
            prepare,
            [(grows, packed[1])] + [(n, rows) for n in sizes] + [(n, columns) for n in sizes] * 2 + half_x,
            where,
            pltpu.with_memory_space_constraint(program_init, pltpu.HBM),
            pltpu.with_memory_space_constraint(counts, pltpu.HBM),
            flops=flops,
            any_args=(1, 2),
            scratch=[pltpu.VMEM(program_init.shape, F32), buffer, pltpu.SemaphoreType.DMA, sems],
        )
        sends, program_own, program_other = [list(rest[i * n_chunks : (i + 1) * n_chunks]) for i in range(3)]
        x_other = list(rest[3 * n_chunks :])
        gram_near = exchange(gram_p, "gene", genes, 1)
        nears = [exchange(a, "gene", genes, 1) for a in sends]
        x0, x1, *rest = chain(
            load_own,
            half_x + [(n, rows) for n in sizes] * 2,
            where,
            pltpu.with_memory_space_constraint(counts, pltpu.HBM),
            *program_own,
            *program_other,
            usage_init.T,
            flops=flops,
            any_args=(1,),
            scratch=[buffer, sems],
        )
        x = [[x0, x1], x_other]
        keeps, usage_own = rest[:n_chunks], rest[n_chunks:]
    else:

        def at(a, which, axis):
            size = a.shape[axis] // 2
            return [lax.dynamic_slice_in_dim(a, i * size, size, axis) for i in (which, 1 - which)]

        def chunked(a):
            return [a[i : i + n] for i, n in zip(starts, sizes)]

        x = [at(part, core, 1) for part in at(counts.astype(BF16), half, 0)]
        program_own, program_other = [chunked(a) for a in at(program_init, core, 1)]
        usage_own = chunked(at(usage_init.T, half, 1)[0])
        gram_p = gram(program_own, program_other, False)[0]
        gram_near = exchange(gram_p, "gene", genes, 1)
        nears, keeps = [], []
        for i in range(n_chunks):
            a, b = program_own[i : i + 1], program_other[i : i + 1]
            nears.append(exchange(product(a, b, *x[1], 1), "gene", genes, 1))
            keeps.append(product(a, b, *x[0], 1))

    for iteration in range(ITERS):
        last = iteration == ITERS - 1
        if iteration:
            nears, keeps = [], []
            for i in range(n_chunks):
                a, b = program_own[i : i + 1], program_other[i : i + 1]
                if i == GRAM_AT:
                    gram_p = gram(program_own, program_other, False)[0]
                    gram_near = exchange(gram_p, "gene", genes, 1)
                nears.append(exchange(product(a, b, *x[1], 1), "gene", genes, 1))
                keeps.append(product(a, b, *x[0], 1))
        gram_top = far(add(gram_p, gram_near), "gene", genes, True)
        tops = [far(add(keep, near), "gene", genes, True) for keep, near in zip(keeps, nears)]
        mine = add(*gram_top)
        theirs = exchange(mine, "cell", cells, 1)
        new, other = update(mine, theirs, usage_own, tops, "gene", genes, 1, USAGE_WEIGHTS)
        usage_own, usage_other = new, other

        tops = []
        for i in range(n_chunks):
            a, b = new[i : i + 1], other[i : i + 1]
            if i < n_chunks - 1:
                cut = sizes[i] // 16 * 8
                send = [exchange(part, "cell", cells, 1) for part in product(a, b, x[0][1], x[1][1], 0, cut)]
                keep = product(a, b, x[0][0], x[1][0], 0)
                tops.append(far(add(keep, *send), "cell", cells, False))
                continue
            gram_send, gram_keep = gram(usage_own, usage_other, True)
            gram_near = exchange(gram_send, "cell", cells, 1)
            send = exchange(product(a, b, x[0][1], x[1][1], 0), "cell", cells, 1)
            keep = product(a, b, x[0][0], x[1][0], 0)
            if last:
                usage = join(usage_own, usage_other, 1, half)
            gram_top = far(add(gram_keep, gram_near), "cell", cells, False)
            tops = [(add(*top),) for top in tops]
            tops.append(far(add(keep, send), "cell", cells, False))
        mine = add(*gram_top)
        theirs = exchange(mine, "cell", cells, 1)
        weights = (PROGRAM_WEIGHTS[last], 1, 1)
        program_own, program_other = update(mine, theirs, program_own, tops, "cell", cells, 1, weights)

    return usage.T, join(program_own, program_other, 0, core)


def solution(mesh):
    return jax.shard_map(
        functools.partial(body, mesh.shape["gene"], mesh.shape["cell"]),
        mesh=mesh,
        in_specs=(P("cell", "gene"), P(("rep", "cell"), None), P("rep", "gene")),
        out_specs=(P(("rep", "cell"), None), P("rep", "gene")),
        check_vma=False,
    )
```

```python
import functools

import jax
import jax.numpy as jnp
from jax import lax
from jax.experimental import pallas as pl
from jax.experimental.pallas import tpu as pltpu
from jax.sharding import PartitionSpec as P

ITERS = 2
CHUNKS = (104, 96)
USAGE_WEIGHTS = (1, 6, 1)
GRAM_AT = 1
PROGRAM_WEIGHTS = (1, 16)
VMEM = pl.BlockSpec(memory_space=pltpu.VMEM)
SMEM = pl.BlockSpec(memory_space=pltpu.SMEM)
ANY = pl.BlockSpec(memory_space=pl.ANY)
HBM = pl.BlockSpec(memory_space=pltpu.HBM)
PARAMS = pltpu.CompilerParams(vmem_limit_bytes=16 * 1024 * 1024)
F32 = jnp.float32
BF16 = jnp.bfloat16


def split(a):
    high = a.astype(BF16)
    return high, (a - high.astype(F32)).astype(BF16)


def dot(a, b, a_dim, b_dim):
    return lax.dot_general(a, b, (((a_dim,), (b_dim,)), ((), ())), preferred_element_type=F32)


def dot2(a, b, a_dim, b_dim):
    high, low = split(a)
    return dot(high, b, a_dim, b_dim) + dot(low, b, a_dim, b_dim)


def dot3(a, b, a_dim, b_dim):
    ah, al = split(a)
    bh, bl = split(b)
    return dot(ah, bh, a_dim, b_dim) + (dot(al, bh, a_dim, b_dim) + dot(ah, bl, a_dim, b_dim))


class Chain:
    def __init__(self):
        self.last = None

    def __call__(self, body, outs, *args, flops=0, any_args=(), scratch=()):
        specs = [
            SMEM if a.dtype == jnp.int32 and a.ndim == 1 else HBM if i in any_args else VMEM
            for i, a in enumerate(args)
        ]
        shapes = [s if isinstance(s, jax.ShapeDtypeStruct) else jax.ShapeDtypeStruct(s, F32) for s in outs]
        moved = sum(a.size * a.dtype.itemsize for a in args) + sum(s.size * 4 for s in shapes)
        tail = [] if self.last is None else [self.last]
        n_args = len(args)

        def run(*refs):
            body(*refs[:n_args], *refs[n_args + len(tail) :])

        result = pl.pallas_call(
            run,
            out_shape=[pltpu.VMEM(s.shape, s.dtype) for s in shapes],
            in_specs=specs + [ANY] * len(tail),
            out_specs=[VMEM] * len(outs),
            scratch_shapes=scratch,
            compiler_params=PARAMS,
            cost_estimate=pl.CostEstimate(flops=flops, bytes_accessed=moved, transcendentals=0),
        )(*args, *tail)
        self.last = result[0]
        return result


def exchange(a, axis, size, flip):
    return lax.ppermute(a, axis, [(i, i ^ flip) for i in range(size)])


def body(genes, cells, counts, usage_init, program_init):
    cell, gene = lax.axis_index("cell"), lax.axis_index("gene")
    core = cell % 2
    half = (gene ^ (gene >> 1)) % 2
    n_cells, n_genes = counts.shape
    k = program_init.shape[0]
    rows, columns = n_cells // 2, n_genes // 2
    sizes = []
    while sum(sizes) < k:
        sizes.append(min(CHUNKS[len(sizes)] if len(sizes) < len(CHUNKS) else k, k - sum(sizes)))
    n_chunks = len(sizes)
    starts = [sum(sizes[:i]) for i in range(n_chunks)]
    where = jnp.stack([core, half]).astype(jnp.int32)
    chain = Chain()

    def stacked(refs):
        return jnp.concatenate([r[...] for r in refs], 0)

    lane = 128
    packs = lane < k <= 2 * lane and k % 8 == 0
    packed = (2 * k - lane, lane) if packs else (-(-k // 16) * 16, k)
    grows = packed[0] // 2

    def packed_gram(parts):
        g = sum(dot3(a, a, 1, 1) for a in parts)
        if packs:
            corner = jnp.concatenate([g[lane:, lane:], jnp.zeros((k - lane, 2 * lane - k), F32)], 1)
            return jnp.concatenate([g[:, :lane], corner], 0)
        return jnp.concatenate([g, jnp.zeros((packed[0] - k, k), F32)], 0) if packed[0] > k else g

    def unpacked(t):
        if packs:
            upper = t[lane : 2 * lane].T[:, : k - lane]
            right = jnp.concatenate([upper, t[k:, : k - lane]], 0)
            return jnp.concatenate([t[:k], right], 1)
        return t[:k]

    def share(t, first):
        return jnp.where(first, t[:grows], t[grows:])

    def gram(factor_a, factor_b, both):
        def kernel(where_ref, *refs):
            a_refs, b_refs, outs = refs[:n_chunks], refs[n_chunks : 2 * n_chunks], refs[2 * n_chunks :]
            t = packed_gram([stacked(a_refs), stacked(b_refs)])
            first = where_ref[0] == 0
            if both:
                outs[0][...] = share(t, jnp.logical_not(first))
            outs[-1][...] = share(t, first)

        n = factor_a[0].shape[1] + factor_b[0].shape[1]
        return chain(kernel, [(grows, packed[1])] * (1 + both), where, *factor_a, *factor_b, flops=6 * k * k * n)

    def product(a, b, xa, xb, dim, cut=0):
        parts = len(a)

        def kernel(*refs):
            a_refs, b_refs, (xa_ref, xb_ref, *o_refs) = refs[:parts], refs[parts : 2 * parts], refs[2 * parts :]
            o = dot2(stacked(a_refs), xa_ref[...], 1, dim) + dot2(stacked(b_refs), xb_ref[...], 1, dim)
            if cut:
                o_refs[0][...], o_refs[1][...] = o[:cut], o[cut:]
            else:
                o_refs[0][...] = o

        n, m = sum(r.shape[0] for r in a), xa.shape[1 - dim]
        outs = [(cut, m), (n - cut, m)] if cut else [(n, m)]
        result = chain(kernel, outs, *a, *b, xa, xb, flops=8 * n * a[0].shape[1] * m)
        return result if cut else result[0]

    def add(a, *b):
        def kernel(a_ref, *refs):
            *b_refs, o_ref = refs
            o_ref[...] = a_ref[...] + stacked(b_refs)

        return chain(kernel, [a.shape], a, *b)[0]

    def rows_of(a, index):
        return a[starts[index] : starts[index] + sizes[index]]

    def denominator(where_ref, m_ref, t_ref, f_refs, index):
        own = where_ref[0] == 0
        upper = jnp.where(own, m_ref[...], t_ref[...])
        lower = jnp.where(own, t_ref[...], m_ref[...])
        g = unpacked(jnp.concatenate([upper, lower], 0))
        return dot3(rows_of(g, index), stacked(f_refs), 1, 0)

    def update(mine, theirs, factor, tops, axis, size, flip, weights):
        def first(where_ref, m_ref, t_ref, *refs):
            f_refs, (*top_refs, o_ref) = refs[:n_chunks], refs[n_chunks:]
            below = denominator(where_ref, m_ref, t_ref, f_refs, 0)
            o_ref[...] = f_refs[0][...] * sum(ref[...] for ref in top_refs) / below

        def below(index, where_ref, m_ref, t_ref, *refs):
            refs[-1][...] = denominator(where_ref, m_ref, t_ref, refs[:n_chunks], index)

        def rest(f_ref, d_ref, *refs):
            *top_refs, o_ref = refs
            o_ref[...] = f_ref[...] * sum(ref[...] for ref in top_refs) / d_ref[...]

        m = factor[0].shape[1]
        shapes = [(n, m) for n in sizes]
        flops = [6 * n * k * m * weight for n, weight in zip(sizes, weights)]
        new = [chain(first, shapes[:1], where, mine, theirs, *factor, *tops[0], flops=flops[0])[0]]
        other = [exchange(new[0], axis, size, flip)]
        divisors = [
            chain(functools.partial(below, i), shapes[i : i + 1], where, mine, theirs, *factor)[0]
            for i in range(1, n_chunks)
        ]
        for i in range(1, n_chunks):
            new.append(chain(rest, shapes[i : i + 1], factor[i], divisors[i - 1], *tops[i], flops=flops[i])[0])
            other.append(exchange(new[i], axis, size, flip))
        return new, other

    def join(mine, theirs, index, which):
        size = mine[0].shape[1]
        if size % 128:
            mine, theirs = jnp.concatenate(mine, 0), jnp.concatenate(theirs, 0)
            return jnp.concatenate([jnp.where(which == 0, mine, theirs), jnp.where(which == 0, theirs, mine)], 1)

        def kernel(where_ref, *refs):
            *refs, o_ref = refs
            first = where_ref[index] == 0
            for a, b, start, n in zip(refs[:n_chunks], refs[n_chunks:], starts, sizes):
                o_ref[start : start + n, :size] = jnp.where(first, a[...], b[...])
                o_ref[start : start + n, size:] = jnp.where(first, b[...], a[...])

        return chain(kernel, [(k, 2 * size)], where, *mine, *theirs)[0]

    def far(a, axis, size, mirrored):
        step = 2
        other = jnp.zeros_like(a)
        while step < size:
            if step > 2:
                a = a + other
            other = exchange(a, axis, size, 2 * step - 1 if mirrored else step)
            step *= 2
        return a, other

    if columns % 128 == 0 and rows % 32 == 0:
        pieces = 4
        piece = rows // pieces

        def halves(a, which, size):
            first, second = a[:, :size], a[:, size:]
            return jnp.where(which, second, first), jnp.where(which, first, second)

        def load(start, counts_ref, buffer, sems):
            copies = [
                pltpu.make_async_copy(
                    counts_ref.at[pl.ds(pl.multiple_of(start + i * piece, 8), piece)], buffer.at[i], sems.at[i]
                )
                for i in range(pieces)
            ]
            for copy in copies:
                copy.start()
            return copies

        def convert(copies, swap, x_refs, buffer):
            for i, copy in enumerate(copies):
                copy.wait()
                for x_ref, start in zip(x_refs, (swap * columns, (1 - swap) * columns)):
                    part = buffer[i, :, pl.ds(pl.multiple_of(start, 128), columns)]
                    x_ref[i * piece : (i + 1) * piece, :] = part.astype(F32).astype(BF16)

        def scatter(a, refs):
            for start, n, ref in zip(starts, sizes, refs):
                ref[...] = a[start : start + n]

        def prepare(where_ref, p_ref, counts_ref, *refs):
            s_refs, a_refs, b_refs = [refs[i * n_chunks : (i + 1) * n_chunks] for i in range(3)]
            x0, x1, p, buffer, p_sem, sems = refs[3 * n_chunks :]
            copy = pltpu.make_async_copy(p_ref, p, p_sem)
            copy.start()
            copies = load((1 - where_ref[1]) * rows, counts_ref, buffer, sems)
            copy.wait()
            own, other = halves(p[...], where_ref[0] == 1, columns)
            scatter(own, a_refs)
            scatter(other, b_refs)
            convert(copies, where_ref[0], (x0, x1), buffer)
            scatter(dot2(own, x0[...], 1, 1) + dot2(other, x1[...], 1, 1), s_refs)

        def load_own(where_ref, counts_ref, *refs):
            a_refs, b_refs = refs[:n_chunks], refs[n_chunks : 2 * n_chunks]
            u_ref, *refs = refs[2 * n_chunks :]
            g_ref, x0, x1, *refs = refs
            k_refs, u_refs, (buffer, sems) = refs[:n_chunks], refs[n_chunks : 2 * n_chunks], refs[2 * n_chunks :]
            copies = load(where_ref[1] * rows, counts_ref, buffer, sems)
            own, other = stacked(a_refs), stacked(b_refs)
            g_ref[...] = share(packed_gram([own, other]), where_ref[0] == 0)
            mine, _ = halves(u_ref[...], where_ref[1] == 1, rows)
            scatter(mine, u_refs)
            convert(copies, where_ref[0], (x0, x1), buffer)
            scatter(dot2(own, x0[...], 1, 1) + dot2(other, x1[...], 1, 1), k_refs)

        half_x = [jax.ShapeDtypeStruct((rows, columns), BF16)] * 2
        buffer = pltpu.VMEM((pieces, piece, n_genes), jnp.int32)
        sems = pltpu.SemaphoreType.DMA((pieces,))
        flops = 4 * k * rows * n_genes
        rest = chain(
            prepare,
            [(n, rows) for n in sizes] + [(n, columns) for n in sizes] * 2 + half_x,
            where,
            pltpu.with_memory_space_constraint(program_init, pltpu.HBM),
            pltpu.with_memory_space_constraint(counts, pltpu.HBM),
            flops=flops,
            any_args=(1, 2),
            scratch=[pltpu.VMEM(program_init.shape, F32), buffer, pltpu.SemaphoreType.DMA, sems],
        )
        sends, program_own, program_other = [list(rest[i * n_chunks : (i + 1) * n_chunks]) for i in range(3)]
        x_other = list(rest[3 * n_chunks :])
        nears = [exchange(a, "gene", genes, 1) for a in sends]
        gram_p, x0, x1, *rest = chain(
            load_own,
            [(grows, packed[1])] + half_x + [(n, rows) for n in sizes] * 2,
            where,
            pltpu.with_memory_space_constraint(counts, pltpu.HBM),
            *program_own,
            *program_other,
            usage_init.T,
            flops=flops,
            any_args=(1,),
            scratch=[buffer, sems],
        )
        x = [[x0, x1], x_other]
        keeps, usage_own = rest[:n_chunks], rest[n_chunks:]
        gram_near = exchange(gram_p, "gene", genes, 1)
    else:

        def at(a, which, axis):
            size = a.shape[axis] // 2
            return [lax.dynamic_slice_in_dim(a, i * size, size, axis) for i in (which, 1 - which)]

        def chunked(a):
            return [a[i : i + n] for i, n in zip(starts, sizes)]

        x = [at(part, core, 1) for part in at(counts.astype(BF16), half, 0)]
        program_own, program_other = [chunked(a) for a in at(program_init, core, 1)]
        usage_own = chunked(at(usage_init.T, half, 1)[0])
        gram_p = gram(program_own, program_other, False)[0]
        gram_near = exchange(gram_p, "gene", genes, 1)
        nears, keeps = [], []
        for i in range(n_chunks):
            a, b = program_own[i : i + 1], program_other[i : i + 1]
            nears.append(exchange(product(a, b, *x[1], 1), "gene", genes, 1))
            keeps.append(product(a, b, *x[0], 1))

    for iteration in range(ITERS):
        last = iteration == ITERS - 1
        if iteration:
            nears, keeps = [], []
            for i in range(n_chunks):
                a, b = program_own[i : i + 1], program_other[i : i + 1]
                if i == GRAM_AT:
                    gram_p = gram(program_own, program_other, False)[0]
                    gram_near = exchange(gram_p, "gene", genes, 1)
                nears.append(exchange(product(a, b, *x[1], 1), "gene", genes, 1))
                keeps.append(product(a, b, *x[0], 1))
        gram_top = far(add(gram_p, gram_near), "gene", genes, True)
        tops = [far(add(keep, near), "gene", genes, True) for keep, near in zip(keeps, nears)]
        mine = add(*gram_top)
        theirs = exchange(mine, "cell", cells, 1)
        new, other = update(mine, theirs, usage_own, tops, "gene", genes, 1, USAGE_WEIGHTS)
        usage_own, usage_other = new, other

        tops = []
        for i in range(n_chunks):
            a, b = new[i : i + 1], other[i : i + 1]
            if i < n_chunks - 1:
                cut = sizes[i] // 16 * 8
                send = [exchange(part, "cell", cells, 1) for part in product(a, b, x[0][1], x[1][1], 0, cut)]
                keep = product(a, b, x[0][0], x[1][0], 0)
                tops.append(far(add(keep, *send), "cell", cells, False))
                continue
            gram_send, gram_keep = gram(usage_own, usage_other, True)
            gram_near = exchange(gram_send, "cell", cells, 1)
            send = exchange(product(a, b, x[0][1], x[1][1], 0), "cell", cells, 1)
            keep = product(a, b, x[0][0], x[1][0], 0)
            if last:
                usage = join(usage_own, usage_other, 1, half)
            gram_top = far(add(gram_keep, gram_near), "cell", cells, False)
            tops = [(add(*top),) for top in tops]
            tops.append(far(add(keep, send), "cell", cells, False))
        mine = add(*gram_top)
        theirs = exchange(mine, "cell", cells, 1)
        weights = (PROGRAM_WEIGHTS[last], 1, 1)
        program_own, program_other = update(mine, theirs, program_own, tops, "cell", cells, 1, weights)

    return usage.T, join(program_own, program_other, 0, core)


def solution(mesh):
    return jax.shard_map(
        functools.partial(body, mesh.shape["gene"], mesh.shape["cell"]),
        mesh=mesh,
        in_specs=(P("cell", "gene"), P(("rep", "cell"), None), P("rep", "gene")),
        out_specs=(P(("rep", "cell"), None), P("rep", "gene")),
        check_vma=False,
    )
```

```python
import functools

import jax
import jax.numpy as jnp
from jax import lax
from jax.experimental import pallas as pl
from jax.experimental.pallas import tpu as pltpu
from jax.sharding import PartitionSpec as P

ITERS = 2
CHUNKS = (104, 96)
USAGE_WEIGHTS = (1, 6, 1)
GRAM_AT = 1
PROGRAM_WEIGHTS = (1, 16)
VMEM = pl.BlockSpec(memory_space=pltpu.VMEM)
SMEM = pl.BlockSpec(memory_space=pltpu.SMEM)
ANY = pl.BlockSpec(memory_space=pl.ANY)
HBM = pl.BlockSpec(memory_space=pltpu.HBM)
PARAMS = pltpu.CompilerParams(vmem_limit_bytes=16 * 1024 * 1024)
F32 = jnp.float32
BF16 = jnp.bfloat16


def split(a):
    high = a.astype(BF16)
    return high, (a - high.astype(F32)).astype(BF16)


def dot(a, b, a_dim, b_dim):
    return lax.dot_general(a, b, (((a_dim,), (b_dim,)), ((), ())), preferred_element_type=F32)


def dot2(a, b, a_dim, b_dim):
    high, low = split(a)
    return dot(high, b, a_dim, b_dim) + dot(low, b, a_dim, b_dim)


def dot3(a, b, a_dim, b_dim):
    ah, al = split(a)
    bh, bl = split(b)
    return dot(ah, bh, a_dim, b_dim) + (dot(al, bh, a_dim, b_dim) + dot(ah, bl, a_dim, b_dim))


class Chain:
    def __init__(self):
        self.last = None

    def __call__(self, body, outs, *args, flops=0, any_args=(), scratch=()):
        specs = [
            SMEM if a.dtype == jnp.int32 and a.ndim == 1 else HBM if i in any_args else VMEM
            for i, a in enumerate(args)
        ]
        shapes = [s if isinstance(s, jax.ShapeDtypeStruct) else jax.ShapeDtypeStruct(s, F32) for s in outs]
        moved = sum(a.size * a.dtype.itemsize for a in args) + sum(s.size * 4 for s in shapes)
        tail = [] if self.last is None else [self.last]
        n_args = len(args)

        def run(*refs):
            body(*refs[:n_args], *refs[n_args + len(tail) :])

        result = pl.pallas_call(
            run,
            out_shape=[pltpu.VMEM(s.shape, s.dtype) for s in shapes],
            in_specs=specs + [ANY] * len(tail),
            out_specs=[VMEM] * len(outs),
            scratch_shapes=scratch,
            compiler_params=PARAMS,
            cost_estimate=pl.CostEstimate(flops=flops, bytes_accessed=moved, transcendentals=0),
        )(*args, *tail)
        self.last = result[0]
        return result


def exchange(a, axis, size, flip):
    return lax.ppermute(a, axis, [(i, i ^ flip) for i in range(size)])


def body(genes, cells, counts, usage_init, program_init):
    cell, gene = lax.axis_index("cell"), lax.axis_index("gene")
    core = cell % 2
    half = (gene ^ (gene >> 1)) % 2
    n_cells, n_genes = counts.shape
    k = program_init.shape[0]
    rows, columns = n_cells // 2, n_genes // 2
    sizes = []
    while sum(sizes) < k:
        sizes.append(min(CHUNKS[len(sizes)] if len(sizes) < len(CHUNKS) else k, k - sum(sizes)))
    n_chunks = len(sizes)
    starts = [sum(sizes[:i]) for i in range(n_chunks)]
    where = jnp.stack([core, half]).astype(jnp.int32)
    chain = Chain()

    def stacked(refs):
        return jnp.concatenate([r[...] for r in refs], 0)

    lane = 128
    packs = lane < k <= 2 * lane and k % 8 == 0
    packed = (2 * k - lane, lane) if packs else (-(-k // 16) * 16, k)
    grows = packed[0] // 2

    def packed_gram(parts):
        g = sum(dot3(a, a, 1, 1) for a in parts)
        if packs:
            corner = jnp.concatenate([g[lane:, lane:], jnp.zeros((k - lane, 2 * lane - k), F32)], 1)
            return jnp.concatenate([g[:, :lane], corner], 0)
        return jnp.concatenate([g, jnp.zeros((packed[0] - k, k), F32)], 0) if packed[0] > k else g

    def unpacked(t):
        if packs:
            upper = t[lane : 2 * lane].T[:, : k - lane]
            right = jnp.concatenate([upper, t[k:, : k - lane]], 0)
            return jnp.concatenate([t[:k], right], 1)
        return t[:k]

    def share(t, first):
        return jnp.where(first, t[:grows], t[grows:])

    def gram(factor_a, factor_b, both):
        def kernel(where_ref, *refs):
            a_refs, b_refs, outs = refs[:n_chunks], refs[n_chunks : 2 * n_chunks], refs[2 * n_chunks :]
            t = packed_gram([stacked(a_refs), stacked(b_refs)])
            first = where_ref[0] == 0
            if both:
                outs[0][...] = share(t, jnp.logical_not(first))
            outs[-1][...] = share(t, first)

        n = factor_a[0].shape[1] + factor_b[0].shape[1]
        return chain(kernel, [(grows, packed[1])] * (1 + both), where, *factor_a, *factor_b, flops=6 * k * k * n)

    def partial(a, xa, dim):
        def kernel(a_ref, xa_ref, o_ref):
            o_ref[...] = dot2(a_ref[...], xa_ref[...], 1, dim)

        return chain(kernel, [(a.shape[0], xa.shape[1 - dim])], a, xa)[0]

    def rest_of_product(base, b, xb, dim, cut=0):
        n, m = base.shape

        def kernel(base_ref, b_ref, xb_ref, *o_refs):
            o = base_ref[...] + dot2(b_ref[...], xb_ref[...], 1, dim)
            for ref, part in zip(o_refs, (o[:cut], o[cut:]) if cut else (o,)):
                ref[...] = part

        outs = [(cut, m), (n - cut, m)] if cut else [(n, m)]
        return chain(kernel, outs, base, b, xb, flops=8 * n * b.shape[1] * m)

    def product(a, b, xa, xb, dim, cut=0):
        parts = len(a)

        def kernel(*refs):
            a_refs, b_refs, (xa_ref, xb_ref, *o_refs) = refs[:parts], refs[parts : 2 * parts], refs[2 * parts :]
            o = dot2(stacked(a_refs), xa_ref[...], 1, dim) + dot2(stacked(b_refs), xb_ref[...], 1, dim)
            if cut:
                o_refs[0][...], o_refs[1][...] = o[:cut], o[cut:]
            else:
                o_refs[0][...] = o

        n, m = sum(r.shape[0] for r in a), xa.shape[1 - dim]
        outs = [(cut, m), (n - cut, m)] if cut else [(n, m)]
        result = chain(kernel, outs, *a, *b, xa, xb, flops=8 * n * a[0].shape[1] * m)
        return result if cut else result[0]

    def add(a, *b):
        def kernel(a_ref, *refs):
            *b_refs, o_ref = refs
            o_ref[...] = a_ref[...] + stacked(b_refs)

        return chain(kernel, [a.shape], a, *b)[0]

    def rows_of(a, index):
        return a[starts[index] : starts[index] + sizes[index]]

    def denominator(where_ref, m_ref, t_ref, f_refs, index):
        own = where_ref[0] == 0
        upper = jnp.where(own, m_ref[...], t_ref[...])
        lower = jnp.where(own, t_ref[...], m_ref[...])
        g = unpacked(jnp.concatenate([upper, lower], 0))
        return dot3(rows_of(g, index), stacked(f_refs), 1, 0)

    def update(mine, theirs, factor, tops, axis, size, flip, weights, x_next, dim):
        def first(where_ref, m_ref, t_ref, *refs):
            f_refs, (*top_refs, o_ref) = refs[:n_chunks], refs[n_chunks:]
            below = denominator(where_ref, m_ref, t_ref, f_refs, 0)
            o_ref[...] = f_refs[0][...] * sum(ref[...] for ref in top_refs) / below

        def below(index, where_ref, m_ref, t_ref, *refs):
            refs[-1][...] = denominator(where_ref, m_ref, t_ref, refs[:n_chunks], index)

        def rest(f_ref, d_ref, *refs):
            *top_refs, o_ref = refs
            o_ref[...] = f_ref[...] * sum(ref[...] for ref in top_refs) / d_ref[...]

        m = factor[0].shape[1]
        shapes = [(n, m) for n in sizes]
        flops = [6 * n * k * m * weight for n, weight in zip(sizes, weights)]
        new = [chain(first, shapes[:1], where, mine, theirs, *factor, *tops[0], flops=flops[0])[0]]
        other = [exchange(new[0], axis, size, flip)]
        divisors = [
            chain(functools.partial(below, i), shapes[i : i + 1], where, mine, theirs, *factor)[0]
            for i in range(1, n_chunks)
        ]
        base = None if x_next is None else partial(new[0], x_next, dim)
        for i in range(1, n_chunks):
            new.append(chain(rest, shapes[i : i + 1], factor[i], divisors[i - 1], *tops[i], flops=flops[i])[0])
            other.append(exchange(new[i], axis, size, flip))
        return new, other, base

    def join(mine, theirs, index, which):
        size = mine[0].shape[1]
        if size % 128:
            mine, theirs = jnp.concatenate(mine, 0), jnp.concatenate(theirs, 0)
            return jnp.concatenate([jnp.where(which == 0, mine, theirs), jnp.where(which == 0, theirs, mine)], 1)

        def kernel(where_ref, *refs):
            *refs, o_ref = refs
            first = where_ref[index] == 0
            for a, b, start, n in zip(refs[:n_chunks], refs[n_chunks:], starts, sizes):
                o_ref[start : start + n, :size] = jnp.where(first, a[...], b[...])
                o_ref[start : start + n, size:] = jnp.where(first, b[...], a[...])

        return chain(kernel, [(k, 2 * size)], where, *mine, *theirs)[0]

    def far(a, axis, size, mirrored):
        step = 2
        other = jnp.zeros_like(a)
        while step < size:
            if step > 2:
                a = a + other
            other = exchange(a, axis, size, 2 * step - 1 if mirrored else step)
            step *= 2
        return a, other

    if columns % 128 == 0 and rows % 32 == 0:
        pieces = 4
        piece = rows // pieces

        def halves(a, which, size):
            first, second = a[:, :size], a[:, size:]
            return jnp.where(which, second, first), jnp.where(which, first, second)

        def load(start, counts_ref, buffer, sems):
            copies = [
                pltpu.make_async_copy(
                    counts_ref.at[pl.ds(pl.multiple_of(start + i * piece, 8), piece)], buffer.at[i], sems.at[i]
                )
                for i in range(pieces)
            ]
            for copy in copies:
                copy.start()
            return copies

        def convert(copies, swap, x_refs, buffer):
            for i, copy in enumerate(copies):
                copy.wait()
                for x_ref, start in zip(x_refs, (swap * columns, (1 - swap) * columns)):
                    part = buffer[i, :, pl.ds(pl.multiple_of(start, 128), columns)]
                    x_ref[i * piece : (i + 1) * piece, :] = part.astype(F32).astype(BF16)

        def scatter(a, refs):
            for start, n, ref in zip(starts, sizes, refs):
                ref[...] = a[start : start + n]

        def prepare(where_ref, p_ref, counts_ref, *refs):
            s_refs, a_refs, b_refs = [refs[i * n_chunks : (i + 1) * n_chunks] for i in range(3)]
            x0, x1, p, buffer, p_sem, sems = refs[3 * n_chunks :]
            copy = pltpu.make_async_copy(p_ref, p, p_sem)
            copy.start()
            copies = load((1 - where_ref[1]) * rows, counts_ref, buffer, sems)
            copy.wait()
            own, other = halves(p[...], where_ref[0] == 1, columns)
            scatter(own, a_refs)
            scatter(other, b_refs)
            convert(copies, where_ref[0], (x0, x1), buffer)
            scatter(dot2(own, x0[...], 1, 1) + dot2(other, x1[...], 1, 1), s_refs)

        def load_own(where_ref, counts_ref, *refs):
            a_refs, b_refs = refs[:n_chunks], refs[n_chunks : 2 * n_chunks]
            u_ref, *refs = refs[2 * n_chunks :]
            g_ref, x0, x1, *refs = refs
            k_refs, u_refs, (buffer, sems) = refs[:n_chunks], refs[n_chunks : 2 * n_chunks], refs[2 * n_chunks :]
            copies = load(where_ref[1] * rows, counts_ref, buffer, sems)
            own, other = stacked(a_refs), stacked(b_refs)
            g_ref[...] = share(packed_gram([own, other]), where_ref[0] == 0)
            mine, _ = halves(u_ref[...], where_ref[1] == 1, rows)
            scatter(mine, u_refs)
            convert(copies, where_ref[0], (x0, x1), buffer)
            scatter(dot2(own, x0[...], 1, 1) + dot2(other, x1[...], 1, 1), k_refs)

        half_x = [jax.ShapeDtypeStruct((rows, columns), BF16)] * 2
        buffer = pltpu.VMEM((pieces, piece, n_genes), jnp.int32)
        sems = pltpu.SemaphoreType.DMA((pieces,))
        flops = 4 * k * rows * n_genes
        rest = chain(
            prepare,
            [(n, rows) for n in sizes] + [(n, columns) for n in sizes] * 2 + half_x,
            where,
            pltpu.with_memory_space_constraint(program_init, pltpu.HBM),
            pltpu.with_memory_space_constraint(counts, pltpu.HBM),
            flops=flops,
            any_args=(1, 2),
            scratch=[pltpu.VMEM(program_init.shape, F32), buffer, pltpu.SemaphoreType.DMA, sems],
        )
        sends, program_own, program_other = [list(rest[i * n_chunks : (i + 1) * n_chunks]) for i in range(3)]
        x_other = list(rest[3 * n_chunks :])
        nears = [exchange(a, "gene", genes, 1) for a in sends]
        gram_p, x0, x1, *rest = chain(
            load_own,
            [(grows, packed[1])] + half_x + [(n, rows) for n in sizes] * 2,
            where,
            pltpu.with_memory_space_constraint(counts, pltpu.HBM),
            *program_own,
            *program_other,
            usage_init.T,
            flops=flops,
            any_args=(1,),
            scratch=[buffer, sems],
        )
        x = [[x0, x1], x_other]
        keeps, usage_own = rest[:n_chunks], rest[n_chunks:]
        gram_near = exchange(gram_p, "gene", genes, 1)
    else:

        def at(a, which, axis):
            size = a.shape[axis] // 2
            return [lax.dynamic_slice_in_dim(a, i * size, size, axis) for i in (which, 1 - which)]

        def chunked(a):
            return [a[i : i + n] for i, n in zip(starts, sizes)]

        x = [at(part, core, 1) for part in at(counts.astype(BF16), half, 0)]
        program_own, program_other = [chunked(a) for a in at(program_init, core, 1)]
        usage_own = chunked(at(usage_init.T, half, 1)[0])
        gram_p = gram(program_own, program_other, False)[0]
        gram_near = exchange(gram_p, "gene", genes, 1)
        nears, keeps = [], []
        for i in range(n_chunks):
            a, b = program_own[i : i + 1], program_other[i : i + 1]
            nears.append(exchange(product(a, b, *x[1], 1), "gene", genes, 1))
            keeps.append(product(a, b, *x[0], 1))

    for iteration in range(ITERS):
        last = iteration == ITERS - 1
        if iteration:
            nears, keeps = [], []
            for i in range(n_chunks):
                a, b = program_own[i : i + 1], program_other[i : i + 1]
                if i == GRAM_AT:
                    gram_p = gram(program_own, program_other, False)[0]
                    gram_near = exchange(gram_p, "gene", genes, 1)
                send = product(a, b, *x[1], 1) if i else rest_of_product(base, b[0], x[1][1], 1)[0]
                nears.append(exchange(send, "gene", genes, 1))
                keeps.append(product(a, b, *x[0], 1))
        gram_top = far(add(gram_p, gram_near), "gene", genes, True)
        tops = [far(add(keep, near), "gene", genes, True) for keep, near in zip(keeps, nears)]
        mine = add(*gram_top)
        theirs = exchange(mine, "cell", cells, 1)
        new, other, base = update(mine, theirs, usage_own, tops, "gene", genes, 1, USAGE_WEIGHTS, x[0][1], 0)
        usage_own, usage_other = new, other

        tops = []
        for i in range(n_chunks):
            a, b = new[i : i + 1], other[i : i + 1]
            if i < n_chunks - 1:
                cut = sizes[i] // 16 * 8
                if i:
                    send = product(a, b, x[0][1], x[1][1], 0, cut)
                else:
                    send = rest_of_product(base, b[0], x[1][1], 0, cut)
                send = [exchange(part, "cell", cells, 1) for part in send]
                keep = product(a, b, x[0][0], x[1][0], 0)
                tops.append(far(add(keep, *send), "cell", cells, False))
                continue
            gram_send, gram_keep = gram(usage_own, usage_other, True)
            gram_near = exchange(gram_send, "cell", cells, 1)
            send = exchange(product(a, b, x[0][1], x[1][1], 0), "cell", cells, 1)
            keep = product(a, b, x[0][0], x[1][0], 0)
            if last:
                usage = join(usage_own, usage_other, 1, half)
            gram_top = far(add(gram_keep, gram_near), "cell", cells, False)
            tops = [(add(*top),) for top in tops]
            tops.append(far(add(keep, send), "cell", cells, False))
        mine = add(*gram_top)
        theirs = exchange(mine, "cell", cells, 1)
        weights = (PROGRAM_WEIGHTS[last], 1, 1)
        x_next = None if last else x[1][0]
        program_own, program_other, base = update(
            mine, theirs, program_own, tops, "cell", cells, 1, weights, x_next, 1
        )

    return usage.T, join(program_own, program_other, 0, core)


def solution(mesh):
    return jax.shard_map(
        functools.partial(body, mesh.shape["gene"], mesh.shape["cell"]),
        mesh=mesh,
        in_specs=(P("cell", "gene"), P(("rep", "cell"), None), P("rep", "gene")),
        out_specs=(P(("rep", "cell"), None), P("rep", "gene")),
        check_vma=False,
    )
```

```python
import functools

import jax
import jax.numpy as jnp
from jax import lax
from jax.experimental import pallas as pl
from jax.experimental.pallas import tpu as pltpu
from jax.sharding import PartitionSpec as P

ITERS = 2
CHUNKS = (104, 96)
USAGE_WEIGHTS = (1, 6, 1)
GRAM_AT = 1
PROGRAM_WEIGHTS = (1, 16)
VMEM = pl.BlockSpec(memory_space=pltpu.VMEM)
SMEM = pl.BlockSpec(memory_space=pltpu.SMEM)
ANY = pl.BlockSpec(memory_space=pl.ANY)
HBM = pl.BlockSpec(memory_space=pltpu.HBM)
PARAMS = pltpu.CompilerParams(vmem_limit_bytes=16 * 1024 * 1024)
F32 = jnp.float32
BF16 = jnp.bfloat16


def split(a):
    high = a.astype(BF16)
    return high, (a - high.astype(F32)).astype(BF16)


def dot(a, b, a_dim, b_dim):
    return lax.dot_general(a, b, (((a_dim,), (b_dim,)), ((), ())), preferred_element_type=F32)


def dot2(a, b, a_dim, b_dim):
    high, low = split(a)
    return dot(high, b, a_dim, b_dim) + dot(low, b, a_dim, b_dim)


def dot3(a, b, a_dim, b_dim):
    ah, al = split(a)
    bh, bl = split(b)
    return dot(ah, bh, a_dim, b_dim) + (dot(al, bh, a_dim, b_dim) + dot(ah, bl, a_dim, b_dim))


class Chain:
    def __init__(self):
        self.last = None

    def __call__(self, body, outs, *args, flops=0, any_args=(), scratch=()):
        specs = [
            SMEM if a.dtype == jnp.int32 and a.ndim == 1 else HBM if i in any_args else VMEM
            for i, a in enumerate(args)
        ]
        shapes = [s if isinstance(s, jax.ShapeDtypeStruct) else jax.ShapeDtypeStruct(s, F32) for s in outs]
        moved = sum(a.size * a.dtype.itemsize for a in args) + sum(s.size * 4 for s in shapes)
        tail = [] if self.last is None else [self.last]
        n_args = len(args)

        def run(*refs):
            body(*refs[:n_args], *refs[n_args + len(tail) :])

        result = pl.pallas_call(
            run,
            out_shape=[pltpu.VMEM(s.shape, s.dtype) for s in shapes],
            in_specs=specs + [ANY] * len(tail),
            out_specs=[VMEM] * len(outs),
            scratch_shapes=scratch,
            compiler_params=PARAMS,
            cost_estimate=pl.CostEstimate(flops=flops, bytes_accessed=moved, transcendentals=0),
        )(*args, *tail)
        self.last = result[0]
        return result


def exchange(a, axis, size, flip):
    return lax.ppermute(a, axis, [(i, i ^ flip) for i in range(size)])


def body(genes, cells, counts, usage_init, program_init):
    cell, gene = lax.axis_index("cell"), lax.axis_index("gene")
    core = cell % 2
    half = (gene ^ (gene >> 1)) % 2
    n_cells, n_genes = counts.shape
    k = program_init.shape[0]
    rows, columns = n_cells // 2, n_genes // 2
    sizes = []
    while sum(sizes) < k:
        sizes.append(min(CHUNKS[len(sizes)] if len(sizes) < len(CHUNKS) else k, k - sum(sizes)))
    n_chunks = len(sizes)
    starts = [sum(sizes[:i]) for i in range(n_chunks)]
    where = jnp.stack([core, half]).astype(jnp.int32)
    chain = Chain()

    def stacked(refs):
        return jnp.concatenate([r[...] for r in refs], 0)

    lane = 128
    packs = lane < k <= 2 * lane and k % 8 == 0
    packed = (2 * k - lane, lane) if packs else (-(-k // 16) * 16, k)
    grows = packed[0] // 2

    def packed_gram(parts):
        g = sum(dot3(a, a, 1, 1) for a in parts)
        if packs:
            corner = jnp.concatenate([g[lane:, lane:], jnp.zeros((k - lane, 2 * lane - k), F32)], 1)
            return jnp.concatenate([g[:, :lane], corner], 0)
        return jnp.concatenate([g, jnp.zeros((packed[0] - k, k), F32)], 0) if packed[0] > k else g

    def unpacked(t):
        if packs:
            upper = t[lane : 2 * lane].T[:, : k - lane]
            right = jnp.concatenate([upper, t[k:, : k - lane]], 0)
            return jnp.concatenate([t[:k], right], 1)
        return t[:k]

    def share(t, first):
        return jnp.where(first, t[:grows], t[grows:])

    def gram(factor_a, factor_b, both):
        def kernel(where_ref, *refs):
            a_refs, b_refs, outs = refs[:n_chunks], refs[n_chunks : 2 * n_chunks], refs[2 * n_chunks :]
            t = packed_gram([stacked(a_refs), stacked(b_refs)])
            first = where_ref[0] == 0
            if both:
                outs[0][...] = share(t, jnp.logical_not(first))
            outs[-1][...] = share(t, first)

        n = factor_a[0].shape[1] + factor_b[0].shape[1]
        return chain(kernel, [(grows, packed[1])] * (1 + both), where, *factor_a, *factor_b, flops=6 * k * k * n)

    def partial(a, xa, dim):
        def kernel(a_ref, xa_ref, o_ref):
            o_ref[...] = dot2(a_ref[...], xa_ref[...], 1, dim)

        return chain(kernel, [(a.shape[0], xa.shape[1 - dim])], a, xa)[0]

    def rest_of_product(base, b, xb, dim, cut=0):
        n, m = base.shape

        def kernel(base_ref, b_ref, xb_ref, *o_refs):
            o = base_ref[...] + dot2(b_ref[...], xb_ref[...], 1, dim)
            for ref, part in zip(o_refs, (o[:cut], o[cut:]) if cut else (o,)):
                ref[...] = part

        outs = [(cut, m), (n - cut, m)] if cut else [(n, m)]
        return chain(kernel, outs, base, b, xb, flops=8 * n * b.shape[1] * m)

    def product(a, b, xa, xb, dim, cut=0):
        parts = len(a)

        def kernel(*refs):
            a_refs, b_refs, (xa_ref, xb_ref, *o_refs) = refs[:parts], refs[parts : 2 * parts], refs[2 * parts :]
            o = dot2(stacked(a_refs), xa_ref[...], 1, dim) + dot2(stacked(b_refs), xb_ref[...], 1, dim)
            if cut:
                o_refs[0][...], o_refs[1][...] = o[:cut], o[cut:]
            else:
                o_refs[0][...] = o

        n, m = sum(r.shape[0] for r in a), xa.shape[1 - dim]
        outs = [(cut, m), (n - cut, m)] if cut else [(n, m)]
        result = chain(kernel, outs, *a, *b, xa, xb, flops=8 * n * a[0].shape[1] * m)
        return result if cut else result[0]

    def add(a, *b):
        def kernel(a_ref, *refs):
            *b_refs, o_ref = refs
            o_ref[...] = a_ref[...] + stacked(b_refs)

        return chain(kernel, [a.shape], a, *b)[0]

    def rows_of(a, index):
        return a[starts[index] : starts[index] + sizes[index]]

    def denominator(where_ref, m_ref, t_ref, f_refs, index):
        own = where_ref[0] == 0
        upper = jnp.where(own, m_ref[...], t_ref[...])
        lower = jnp.where(own, t_ref[...], m_ref[...])
        g = unpacked(jnp.concatenate([upper, lower], 0))
        return dot3(rows_of(g, index), stacked(f_refs), 1, 0)

    def update(mine, theirs, factor, tops, axis, size, flip, weights, x_next, dim):
        def first(where_ref, m_ref, t_ref, *refs):
            f_refs, (*top_refs, o_ref) = refs[:n_chunks], refs[n_chunks:]
            below = denominator(where_ref, m_ref, t_ref, f_refs, 0)
            o_ref[...] = f_refs[0][...] * sum(ref[...] for ref in top_refs) / below

        def below(index, where_ref, m_ref, t_ref, *refs):
            refs[-1][...] = denominator(where_ref, m_ref, t_ref, refs[:n_chunks], index)

        def rest(f_ref, d_ref, *refs):
            *top_refs, o_ref = refs
            o_ref[...] = f_ref[...] * sum(ref[...] for ref in top_refs) / d_ref[...]

        m = factor[0].shape[1]
        shapes = [(n, m) for n in sizes]
        flops = [6 * n * k * m * weight for n, weight in zip(sizes, weights)]
        new = [chain(first, shapes[:1], where, mine, theirs, *factor, *tops[0], flops=flops[0])[0]]
        other = [exchange(new[0], axis, size, flip)]
        divisors = [
            chain(functools.partial(below, i), shapes[i : i + 1], where, mine, theirs, *factor)[0]
            for i in range(1, n_chunks)
        ]
        base = None if x_next is None else partial(new[0], x_next, dim)
        for i in range(1, n_chunks):
            new.append(chain(rest, shapes[i : i + 1], factor[i], divisors[i - 1], *tops[i], flops=flops[i])[0])
            other.append(exchange(new[i], axis, size, flip))
        return new, other, base

    def join(mine, theirs, index, which):
        size = mine[0].shape[1]
        if size % 128:
            mine, theirs = jnp.concatenate(mine, 0), jnp.concatenate(theirs, 0)
            return jnp.concatenate([jnp.where(which == 0, mine, theirs), jnp.where(which == 0, theirs, mine)], 1)

        def kernel(where_ref, *refs):
            *refs, o_ref = refs
            first = where_ref[index] == 0
            for a, b, start, n in zip(refs[:n_chunks], refs[n_chunks:], starts, sizes):
                o_ref[start : start + n, :size] = jnp.where(first, a[...], b[...])
                o_ref[start : start + n, size:] = jnp.where(first, b[...], a[...])

        return chain(kernel, [(k, 2 * size)], where, *mine, *theirs)[0]

    def far(a, axis, size, mirrored):
        step = 2
        other = jnp.zeros_like(a)
        while step < size:
            if step > 2:
                a = a + other
            other = exchange(a, axis, size, 2 * step - 1 if mirrored else step)
            step *= 2
        return a, other

    if columns % 128 == 0 and rows % 32 == 0:
        pieces = 4
        piece = rows // pieces

        def halves(a, which, size):
            first, second = a[:, :size], a[:, size:]
            return jnp.where(which, second, first), jnp.where(which, first, second)

        def load(start, counts_ref, buffer, sems):
            copies = [
                pltpu.make_async_copy(
                    counts_ref.at[pl.ds(pl.multiple_of(start + i * piece, 8), piece)], buffer.at[i], sems.at[i]
                )
                for i in range(pieces)
            ]
            for copy in copies:
                copy.start()
            return copies

        def convert(copies, swap, x_refs, buffer):
            for i, copy in enumerate(copies):
                copy.wait()
                for x_ref, start in zip(x_refs, (swap * columns, (1 - swap) * columns)):
                    part = buffer[i, :, pl.ds(pl.multiple_of(start, 128), columns)]
                    x_ref[i * piece : (i + 1) * piece, :] = part.astype(F32).astype(BF16)

        def scatter(a, refs):
            for start, n, ref in zip(starts, sizes, refs):
                ref[...] = a[start : start + n]

        def prepare(where_ref, p_ref, counts_ref, *refs):
            s_refs, a_refs, b_refs = [refs[i * n_chunks : (i + 1) * n_chunks] for i in range(3)]
            x0, x1, p, buffer, p_sem, sems = refs[3 * n_chunks :]
            copy = pltpu.make_async_copy(p_ref, p, p_sem)
            copy.start()
            copies = load((1 - where_ref[1]) * rows, counts_ref, buffer, sems)
            copy.wait()
            own, other = halves(p[...], where_ref[0] == 1, columns)
            scatter(own, a_refs)
            scatter(other, b_refs)
            convert(copies, where_ref[0], (x0, x1), buffer)
            scatter(dot2(own, x0[...], 1, 1) + dot2(other, x1[...], 1, 1), s_refs)

        def load_own(where_ref, counts_ref, *refs):
            a_refs, b_refs = refs[:n_chunks], refs[n_chunks : 2 * n_chunks]
            u_ref, *refs = refs[2 * n_chunks :]
            g_ref, x0, x1, *refs = refs
            k_refs, u_refs, (buffer, sems) = refs[:n_chunks], refs[n_chunks : 2 * n_chunks], refs[2 * n_chunks :]
            copies = load(where_ref[1] * rows, counts_ref, buffer, sems)
            own, other = stacked(a_refs), stacked(b_refs)
            g_ref[...] = share(packed_gram([own, other]), where_ref[0] == 0)
            mine, _ = halves(u_ref[...], where_ref[1] == 1, rows)
            scatter(mine, u_refs)
            convert(copies, where_ref[0], (x0, x1), buffer)
            scatter(dot2(own, x0[...], 1, 1) + dot2(other, x1[...], 1, 1), k_refs)

        half_x = [jax.ShapeDtypeStruct((rows, columns), BF16)] * 2
        buffer = pltpu.VMEM((pieces, piece, n_genes), jnp.int32)
        sems = pltpu.SemaphoreType.DMA((pieces,))
        flops = 4 * k * rows * n_genes
        rest = chain(
            prepare,
            [(n, rows) for n in sizes] + [(n, columns) for n in sizes] * 2 + half_x,
            where,
            pltpu.with_memory_space_constraint(program_init, pltpu.HBM),
            pltpu.with_memory_space_constraint(counts, pltpu.HBM),
            flops=flops,
            any_args=(1, 2),
            scratch=[pltpu.VMEM(program_init.shape, F32), buffer, pltpu.SemaphoreType.DMA, sems],
        )
        sends, program_own, program_other = [list(rest[i * n_chunks : (i + 1) * n_chunks]) for i in range(3)]
        x_other = list(rest[3 * n_chunks :])
        nears = [exchange(a, "gene", genes, 1) for a in sends]
        gram_p, x0, x1, *rest = chain(
            load_own,
            [(grows, packed[1])] + half_x + [(n, rows) for n in sizes] * 2,
            where,
            pltpu.with_memory_space_constraint(counts, pltpu.HBM),
            *program_own,
            *program_other,
            usage_init.T,
            flops=flops,
            any_args=(1,),
            scratch=[buffer, sems],
        )
        x = [[x0, x1], x_other]
        keeps, usage_own = rest[:n_chunks], rest[n_chunks:]
        gram_near = exchange(gram_p, "gene", genes, 1)
    else:

        def at(a, which, axis):
            size = a.shape[axis] // 2
            return [lax.dynamic_slice_in_dim(a, i * size, size, axis) for i in (which, 1 - which)]

        def chunked(a):
            return [a[i : i + n] for i, n in zip(starts, sizes)]

        x = [at(part, core, 1) for part in at(counts.astype(BF16), half, 0)]
        program_own, program_other = [chunked(a) for a in at(program_init, core, 1)]
        usage_own = chunked(at(usage_init.T, half, 1)[0])
        gram_p = gram(program_own, program_other, False)[0]
        gram_near = exchange(gram_p, "gene", genes, 1)
        nears, keeps = [], []
        for i in range(n_chunks):
            a, b = program_own[i : i + 1], program_other[i : i + 1]
            nears.append(exchange(product(a, b, *x[1], 1), "gene", genes, 1))
            keeps.append(product(a, b, *x[0], 1))

    for iteration in range(ITERS):
        last = iteration == ITERS - 1
        if iteration:
            nears = []
            for i in range(n_chunks):
                a, b = program_own[i : i + 1], program_other[i : i + 1]
                if i == GRAM_AT:
                    gram_p = gram(program_own, program_other, False)[0]
                    gram_near = exchange(gram_p, "gene", genes, 1)
                send = product(a, b, *x[1], 1) if i else rest_of_product(base, b[0], x[1][1], 1)[0]
                nears.append(exchange(send, "gene", genes, 1))
            keeps = [product(program_own[i : i + 1], program_other[i : i + 1], *x[0], 1) for i in range(n_chunks)]
        gram_top = far(add(gram_p, gram_near), "gene", genes, True)
        tops = [far(add(keep, near), "gene", genes, True) for keep, near in zip(keeps, nears)]
        mine = add(*gram_top)
        theirs = exchange(mine, "cell", cells, 1)
        new, other, base = update(mine, theirs, usage_own, tops, "gene", genes, 1, USAGE_WEIGHTS, x[0][1], 0)
        usage_own, usage_other = new, other

        tops = []
        for i in range(n_chunks):
            a, b = new[i : i + 1], other[i : i + 1]
            if i < n_chunks - 1:
                cut = sizes[i] // 16 * 8
                if i:
                    send = product(a, b, x[0][1], x[1][1], 0, cut)
                else:
                    send = rest_of_product(base, b[0], x[1][1], 0, cut)
                send = [exchange(part, "cell", cells, 1) for part in send]
                keep = product(a, b, x[0][0], x[1][0], 0)
                tops.append(far(add(keep, *send), "cell", cells, False))
                continue
            gram_send, gram_keep = gram(usage_own, usage_other, True)
            gram_near = exchange(gram_send, "cell", cells, 1)
            send = exchange(product(a, b, x[0][1], x[1][1], 0), "cell", cells, 1)
            keep = product(a, b, x[0][0], x[1][0], 0)
            if last:
                usage = join(usage_own, usage_other, 1, half)
            gram_top = far(add(gram_keep, gram_near), "cell", cells, False)
            tops = [(add(*top),) for top in tops]
            tops.append(far(add(keep, send), "cell", cells, False))
        mine = add(*gram_top)
        theirs = exchange(mine, "cell", cells, 1)
        weights = (PROGRAM_WEIGHTS[last], 1, 1)
        x_next = None if last else x[1][0]
        program_own, program_other, base = update(
            mine, theirs, program_own, tops, "cell", cells, 1, weights, x_next, 1
        )

    return usage.T, join(program_own, program_other, 0, core)


def solution(mesh):
    return jax.shard_map(
        functools.partial(body, mesh.shape["gene"], mesh.shape["cell"]),
        mesh=mesh,
        in_specs=(P("cell", "gene"), P(("rep", "cell"), None), P("rep", "gene")),
        out_specs=(P(("rep", "cell"), None), P("rep", "gene")),
        check_vma=False,
    )
```
